128 devices in a mesh: grp: 4 (over y), seq: 32 (over z, x, core).
Axes of the slice: x: 4, y: 4, z: 4, core: 2. Of those that a mesh axis runs over, the one named last changes fastest.
Arguments:
- rows_in: bfloat16 [4, 896, 3072], P('grp', 'seq'), may hold values from -6 to 6
- fresh_qkv: bfloat16 [4, 896, 3, 3072], P('grp', 'seq'), may hold values from -30 to 30
- kv_cache: bfloat16 [4, 4096, 2, 3072], P('grp', 'seq'), may hold values from -6 to 6
- chosen: int32 [4, 896], P('grp', 'seq'), may hold values from 0 to 127, as said below
- counts: int32 [4, 32], P('grp', 'seq'), may hold values from 12 to 28, as said below
- modulation: bfloat16 [4, 4, 3072], P('grp'), may hold values from -3 to 3
- w_up: bfloat16 [3072, 6144], P(None, 'grp'), may hold values from -0.109375 to 0.109375
- b_up: bfloat16 [6144], P('grp'), may hold values from -3 to 3
- w_down: bfloat16 [6144, 3072], P('grp'), may hold values from -0.078125 to 0.078125
- b_down: bfloat16 [3072], replicated, may hold values from -3 to 3
Outputs:
- rows_out: bfloat16 [4, 896, 3072], P('grp', 'seq')
The draws below stay inside these ranges and needn't reach their ends.
Inputs may be any that keep to these rules, and one draw needn't show every extreme that they name: The 32 counts of one request sum to exactly 512; in every request some device has 28 and some has 12. `chosen`: the 28 entries of one device's list are distinct local token indices; the first counts entries name the tokens to refresh, the rest are unused.
All inputs are finite; a program needn't handle non-finite values.
Results may differ from the reference program's by a relative error of at most 0.0042.
Values may be sent and summed in bfloat16 or wider, within the bound.
No kernel may reach another device: no remote copies, remote signals or barrier semaphores. Data moves between devices by JAX's collectives and lax.ppermute only.
A program may use at most 128 MiB of HBM per device.

```python
import jax
import jax.numpy as jnp
from jax import lax

D = 3072
HEAD_DIM = 128
HEADS = 24
FF = 6144
TOK_DEV = 128
SEL_DEV = 16
SPREAD = 4
R_MAX = 28
SLOTS = 896
TOKENS = 4096
REQS = 4
N_SEQ = 32


def draw_counts(key, part):
    key = jax.random.fold_in(key, 11)
    quad_count = N_SEQ // 4
    extra_load = jax.random.randint(key, (REQS, quad_count), 0, SPREAD + 1)
    extra_load = extra_load.at[:, 0].set(SPREAD)
    heavy_load = SEL_DEV + 3 * extra_load
    light_load = SEL_DEV - extra_load
    loads_base = jnp.stack([heavy_load, light_load, light_load, light_load], axis=2).reshape(REQS, N_SEQ)
    order_keys = jax.random.split(jax.random.fold_in(key, 1), REQS)
    orders = jax.vmap(lambda one_key: jax.random.permutation(one_key, N_SEQ))(order_keys)
    return jnp.take_along_axis(loads_base, orders, axis=1).astype(jnp.int32)


def draw_chosen(key, part):
    key = jax.random.fold_in(key, 23)
    shard_keys = jax.random.split(key, REQS * N_SEQ)
    token_lists = jax.vmap(lambda one_key: jax.random.permutation(one_key, TOK_DEV)[:R_MAX])(shard_keys)
    return token_lists.reshape(REQS, SLOTS).astype(jnp.int32)


def draw_fresh_qkv(key, part):
    key = jax.random.fold_in(key, 37)
    first_key = jax.random.fold_in(key, 0)
    values = jnp.clip(jax.random.normal(first_key, (REQS, N_SEQ, R_MAX, 3, D), jnp.float32), -6.0, 6.0)
    return values.reshape(REQS, SLOTS, 3, D).astype(jnp.bfloat16)


def block_levels(stream_key, shape, shards, low, top_value):
    level, own = 1.0, jax.random.fold_in(stream_key, 6)
    for dim, blocks in shards:
        steps = jnp.exp(jax.random.uniform(jax.random.fold_in(own, dim), (blocks,), jnp.float32, low / len(shards), top_value / len(shards)))
        level = level * jnp.repeat(steps, shape[dim] // blocks).reshape([-1 if axis == dim else 1 for axis in range(len(shape))])
    return level


def gaussian(key, dims, scale, reach, cuts=(), kind=jnp.bfloat16):
    entries = jax.random.normal(key, dims, jnp.float32) * scale
    if len(cuts) > 0:
        entries = block_levels(key, dims, cuts, -0.22, 0.18) * entries
    return jnp.clip(entries, min=-reach, max=reach).astype(kind)


def setup_inputs(seed: int = 0) -> dict:
    splits = jax.random.split(jax.random.key(seed), 11)
    return {
        "rows_in": gaussian(splits[0], (REQS, SLOTS, D), 1.0, 6.0, ((0, 4), (1, 32))),
        "fresh_qkv": draw_fresh_qkv(jax.random.fold_in(splits[10], 71), 0),
        "kv_cache": gaussian(splits[2], (REQS, TOKENS, 2, D), 1.0, 6.0, ((0, 4), (1, 32))),
        "chosen": draw_chosen(jax.random.fold_in(splits[10], 71), 0),
        "counts": draw_counts(jax.random.fold_in(splits[10], 71), 0),
        "modulation": gaussian(splits[5], (REQS, 4, D), 0.5, 3.0, ((0, 4),)),
        "w_up": gaussian(splits[6], (D, FF), D ** -0.5, 0.109375, ((1, 4),)),
        "b_up": gaussian(splits[7], (FF,), 0.5, 3.0, ((0, 4),)),
        "w_down": gaussian(splits[8], (FF, D), FF ** -0.5, 0.078125, ((0, 4),)),
        "b_down": gaussian(splits[9], (D,), 0.5, 3.0),
    }


eps_norm = 1e-06

def rounded(value):
    return lax.optimization_barrier(value.astype(jnp.bfloat16)).astype(jnp.float32)

def layer_norm(values):
    center = values - lax.optimization_barrier(jnp.mean(values, axis=-1, keepdims=True))
    spread = lax.optimization_barrier(jnp.mean(center * center, axis=-1, keepdims=True))
    return center * lax.rsqrt(spread + eps_norm)

def patch_one(cache_part, fresh_part, where_part):
    return cache_part.at[where_part].set(fresh_part, mode='drop')

def one_group(rows_in, fresh_qkv, kv_cache, chosen, counts, modulation, w_up, b_up, w_down, b_down):
    live_slot = (jnp.arange(R_MAX)[None, :] < counts[:, None]).reshape(SLOTS)
    target = jnp.where(live_slot, chosen, TOK_DEV).astype(jnp.int32).reshape(N_SEQ, R_MAX)
    patched = jax.vmap(patch_one)(kv_cache.reshape(N_SEQ, TOK_DEV, 2, D), fresh_qkv[:, 1:3].reshape(N_SEQ, R_MAX, 2, D), target)
    queries = fresh_qkv[:, 0].astype(jnp.float32).reshape(SLOTS, HEADS, HEAD_DIM)
    score_scale = HEAD_DIM ** (-0.5)

    def shard_part(shard_id, which):
        taken = lax.dynamic_index_in_dim(patched, shard_id, 0, keepdims=False)[:, which]
        return taken.astype(jnp.float32).reshape(TOK_DEV, HEADS, HEAD_DIM)

    def shard_scores(shard_id):
        return jnp.einsum('qhd,khd->qhk', queries, shard_part(shard_id, 0), precision=lax.Precision.HIGHEST) * score_scale
    shard_ids = jnp.arange(N_SEQ, dtype=jnp.int32)
    row_top = lax.optimization_barrier(jnp.max(lax.map(lambda shard_id: lax.optimization_barrier(jnp.max(shard_scores(shard_id), axis=2)), shard_ids), axis=0))

    def accumulate(running, shard_id):
        mixed_sum, mass_sum = running
        exp_scores = jnp.exp(shard_scores(shard_id) - row_top[:, :, None])
        mixed = jnp.einsum('qhk,khd->qhd', rounded(exp_scores), shard_part(shard_id, 1), precision=lax.Precision.HIGHEST).reshape(SLOTS, D)
        return ((mixed_sum + mixed, mass_sum + lax.optimization_barrier(jnp.sum(exp_scores, axis=2))), None)
    start_sums = (jnp.zeros((SLOTS, D), jnp.float32), jnp.zeros((SLOTS, HEADS), jnp.float32))
    totals, unused = lax.scan(accumulate, start_sums, shard_ids)
    mixed_sum, mass_sum = totals
    attended = (mixed_sum.reshape(SLOTS, HEADS, HEAD_DIM) / mass_sum[:, :, None]).reshape(SLOTS, D)
    shifts = modulation.astype(jnp.float32)
    hidden = rows_in.astype(jnp.float32) + shifts[2] * attended
    normed = (layer_norm(hidden) * (1.0 + shifts[1]) + shifts[0]).astype(jnp.bfloat16)
    lifted = jnp.dot(normed, w_up, preferred_element_type=jnp.float32) + b_up.astype(jnp.float32)
    active = jax.nn.gelu(lifted, approximate=True).astype(jnp.bfloat16)
    feed_out = jnp.dot(active, w_down, preferred_element_type=jnp.float32) + b_down.astype(jnp.float32)
    result = (hidden + shifts[3] * feed_out).astype(jnp.bfloat16)
    return jnp.where(live_slot[:, None], result, jnp.zeros_like(result))

def reference(rows_in, fresh_qkv, kv_cache, chosen, counts, modulation, w_up, b_up, w_down, b_down):
    outputs = []
    for member in range(REQS):
        outputs.append(one_group(rows_in[member], fresh_qkv[member], kv_cache[member], chosen[member], counts[member], modulation[member], w_up, b_up, w_down, b_down))
    return jnp.stack(outputs)
```

```python
import jax
import jax.numpy as jnp
from jax import lax
from jax.experimental import pallas as pl
from jax.experimental.pallas import tpu as pltpu
from jax.sharding import PartitionSpec as P

HEAD_DIM = 128
HEADS_HERE = 3
BLOCK = HEADS_HERE * HEAD_DIM
SLOT_PAD = 32
LOG2E = 1.4426950408889634
EPS = 1e-06
SEQ = ("z", "x", "core")
bf16 = jnp.bfloat16
f32 = jnp.float32
i32 = jnp.int32
MB = 1 << 20


def call(kernel, out_shape, scratch=(), limit=16, smem=(), n_in=None, cost=None, **kw):
    specs = [
        pl.BlockSpec(memory_space=pltpu.SMEM if i in smem else pltpu.VMEM) for i in range(n_in)
    ]
    return pl.pallas_call(
        kernel,
        out_shape=out_shape,
        in_specs=specs,
        scratch_shapes=list(scratch),
        compiler_params=pltpu.CompilerParams(vmem_limit_bytes=limit * MB),
        cost_estimate=cost,
        **kw,
    )


def pack_queries_kernel(q_ref, out_ref):
    rows = q_ref.shape[0]
    for dest in range(32):
        z, x, core = dest // 8, dest // 2 % 4, dest % 2
        group = x if core == 0 else 4 + z
        out_ref[dest, :rows, :] = q_ref[:, group * BLOCK : (group + 1) * BLOCK]
        out_ref[dest, rows:, :] = jnp.zeros((SLOT_PAD - rows, BLOCK), bf16)


def pack_cache_kernel(info_ref, kv_ref, kv_new_ref, chosen_ref, keep_ref, send_ref, patched):
    tokens = kv_ref.shape[0]
    slots = kv_new_ref.shape[1]
    core, ring_x, ring_z, count = info_ref[0], info_ref[1], info_ref[2], info_ref[3]
    token_id = lax.broadcasted_iota(i32, (tokens, slots), 0)
    slot_id = lax.broadcasted_iota(i32, (tokens, slots), 1)
    hit = (token_id == chosen_ref[...]) & (slot_id < count)
    hot = jnp.where(hit, 1.0, 0.0)
    taken = jnp.sum(hot, axis=1, keepdims=True) > 0.5
    hot = hot.astype(bf16)
    old = jnp.swapaxes(kv_ref[...], 0, 1)
    for which in range(2):
        new = jnp.dot(hot, kv_new_ref[which], preferred_element_type=f32)
        patched[which] = jnp.where(taken, new, old[which].astype(f32)).astype(bf16)
    half = 4 * BLOCK
    for k in range(4):
        mine = lax.rem(jnp.where(core == 0, ring_x, ring_z) + k, 4)
        other = lax.rem(jnp.where(core == 0, ring_z, ring_x) + k, 4)
        at_mine = pl.multiple_of(core * half + mine * BLOCK, BLOCK)
        at_other = pl.multiple_of((1 - core) * half + other * BLOCK, BLOCK)
        for which in range(2):
            keep_ref[k, which] = patched[which, :, pl.ds(at_mine, BLOCK)]
            send_ref[k, which] = patched[which, :, pl.ds(at_other, BLOCK)]


def attention_kernel(q_ref, keep_ref, first_ref, r1_ref, r2_ref, r3_ref, out_ref, keys, values_t):
    sources = [keep_ref.at[0], first_ref.at[0]]
    for ref in (r1_ref, r2_ref, r3_ref):
        sources += [ref.at[0], ref.at[1]]
    for i, ref in enumerate(sources):
        keys[i * 128 : (i + 1) * 128, :] = ref[0]
        for h in range(HEADS_HERE):
            cols = slice(h * HEAD_DIM, (h + 1) * HEAD_DIM)
            values_t[h, :, i * 128 : (i + 1) * 128] = ref[1, :, cols].T
    scale = LOG2E * HEAD_DIM**-0.5
    tile = 256
    blocks = tile // SLOT_PAD

    def step(t, _):
        q_all = q_ref[pl.ds(t * blocks, blocks)].reshape(tile, BLOCK)
        for h in range(HEADS_HERE):
            cols = slice(h * HEAD_DIM, (h + 1) * HEAD_DIM)
            scores = lax.dot_general(
                keys[:, cols], q_all[:, cols], (((1,), (1,)), ((), ())), preferred_element_type=f32
            )
            top = jnp.max(scores, axis=0, keepdims=True)
            weights = jnp.exp2((scores - top) * scale)
            mass = jnp.sum(weights, axis=0, keepdims=True)
            mixed = jnp.dot(values_t[h], weights.astype(bf16), preferred_element_type=f32)
            mixed = mixed * (1.0 / mass)
            level = top * scale + jnp.log2(mass)
            p0 = level.astype(bf16).astype(f32)
            rest = level - p0
            p1 = rest.astype(bf16).astype(f32)
            p2 = rest - p1
            for g in range(tile // 128):
                lanes = slice(g * 128, (g + 1) * 128)
                turned = mixed[:, lanes].T
                row = lax.broadcasted_iota(i32, (128, HEAD_DIM), 0) % SLOT_PAD
                turned = jnp.where(row == 28, p0[:, lanes], turned)
                turned = jnp.where(row == 29, p1[:, lanes], turned)
                turned = jnp.where(row == 30, p2[:, lanes], turned)
                out_ref[pl.ds(t * blocks + g * 4, 4), :, cols] = turned.astype(bf16).reshape(
                    4, SLOT_PAD, HEAD_DIM
                )
        return 0

    lax.fori_loop(0, q_ref.shape[0] // blocks, step, 0)


def combine_kernel(info_ref, parts_ref, rows_ref, mod_ref, hidden_ref, normed_ref, levels, turned):
    slots = rows_ref.shape[1]
    heads = 24

    def source(part, group):
        return part * 8 + group * 2 if group < 4 else (group - 4) * 8 + part * 2 + 1

    for part in range(4):
        for group in range(8):
            tail = parts_ref[source(part, group), 24:32, :].astype(f32)
            level = tail[4:5] + tail[5:6] + tail[6:7]
            for h in range(HEADS_HERE):
                at = part * heads + group * HEADS_HERE + h
                levels[at : at + 1, :] = level[:, h * HEAD_DIM : (h + 1) * HEAD_DIM]
    pieces = [levels[p * heads : (p + 1) * heads, :] for p in range(4)]
    top = jnp.maximum(jnp.maximum(pieces[0], pieces[1]), jnp.maximum(pieces[2], pieces[3]))
    weights = [jnp.exp2(piece - top) for piece in pieces]
    total = 1.0 / (weights[0] + weights[1] + weights[2] + weights[3])
    for p in range(4):
        levels[p * heads : (p + 1) * heads, :] = weights[p] * total
    levels[4 * heads :, :] = jnp.zeros((128 - 4 * heads, 128), f32)
    turned[...] = levels[...].T
    mine = turned[pl.ds(pl.multiple_of(info_ref[4] * SLOT_PAD, SLOT_PAD), SLOT_PAD), :]
    shifts = mod_ref[0].astype(f32)
    total_sum = jnp.zeros((SLOT_PAD, 1), f32)
    for group in range(8):
        for h in range(HEADS_HERE):
            head = group * HEADS_HERE + h
            acc = jnp.zeros((SLOT_PAD, HEAD_DIM), f32)
            for part in range(4):
                column = part * heads + head
                block = parts_ref[source(part, group), :, h * HEAD_DIM : (h + 1) * HEAD_DIM]
                acc = acc + mine[:, column : column + 1] * block.astype(f32)
            cols = slice(head * HEAD_DIM, (head + 1) * HEAD_DIM)
            attended = acc[:slots] * shifts[2:3, cols]
            hidden_ref[:slots, cols] = rows_ref[0, :, cols].astype(f32) + attended
    hidden_ref[slots:, :] = jnp.zeros((SLOT_PAD - slots, hidden_ref.shape[1]), f32)
    hidden = hidden_ref[...]
    center = hidden - jnp.mean(hidden, axis=1, keepdims=True)
    spread = jnp.mean(center * center, axis=1, keepdims=True)
    normed = center * lax.rsqrt(spread + EPS) * (1.0 + shifts[1:2]) + shifts[0:1]
    normed_ref[...] = normed.astype(bf16)


def feed_kernel(rows_ref, up_ref, b_up_ref, down_ref, out_ref, acc):
    step = pl.program_id(0)
    lifted = jnp.dot(rows_ref[...], up_ref[...], preferred_element_type=f32)
    lifted = lifted + b_up_ref[...].astype(f32)
    active = jax.nn.gelu(lifted, approximate=True).astype(bf16)
    terms = jnp.dot(active, down_ref[...], preferred_element_type=f32)

    @pl.when(step == 0)
    def _():
        acc[...] = terms

    @pl.when(step > 0)
    def _():
        acc[...] = acc[...] + terms

    @pl.when(step == pl.num_programs(0) - 1)
    def _():
        out_ref[...] = acc[...].astype(bf16)


def feed_forward(rows, w_up, b_up, w_down):
    count, width = rows.shape
    hidden_units = w_up.shape[1]
    tile = 256
    return pl.pallas_call(
        feed_kernel,
        grid=(hidden_units // tile,),
        in_specs=[
            pl.BlockSpec((count, width), lambda i: (0, 0)),
            pl.BlockSpec((width, tile), lambda i: (0, i)),
            pl.BlockSpec((1, tile), lambda i: (0, i)),
            pl.BlockSpec((tile, width), lambda i: (i, 0)),
        ],
        out_specs=pl.BlockSpec((count, width), lambda i: (0, 0)),
        out_shape=jax.ShapeDtypeStruct((count, width), bf16),
        scratch_shapes=[pltpu.VMEM((count, width), f32)],
        compiler_params=pltpu.CompilerParams(vmem_limit_bytes=24 * MB),
    )(rows, w_up, b_up, w_down)


def finish_kernel(info_ref, terms_ref, hidden_ref, mod_ref, b_down_ref, out_ref):
    slots = out_ref.shape[1]
    total = terms_ref[0].astype(f32)
    for p in range(1, 4):
        total = total + terms_ref[p].astype(f32)
    feed_out = total[:slots] + b_down_ref[...].astype(f32)
    result = hidden_ref[:slots] + mod_ref[0, 3:4].astype(f32) * feed_out
    live = lax.broadcasted_iota(i32, result.shape, 0) < info_ref[3]
    out_ref[0] = jnp.where(live, result, 0.0).astype(bf16)


def position(z, x, core):
    return (z % 4) * 8 + (x % 4) * 2 + core


def ring_pairs(k):
    return [
        (position(z, x, c), position(z, x + k, 0) if c == 0 else position(z + k, x, 1))
        for z in range(4)
        for x in range(4)
        for c in range(2)
    ]


def body(rows_in, fresh_qkv, kv_cache, chosen, counts, modulation, w_up, b_up, w_down, b_down):
    shape = jax.ShapeDtypeStruct
    slots, width = rows_in.shape[1], rows_in.shape[2]
    tokens = kv_cache.shape[1]
    core, ring_x, ring_z = (lax.axis_index(a) for a in ("core", "x", "z"))
    me = ring_z * 8 + ring_x * 2 + core
    info = jnp.stack([core, ring_x, ring_z, counts[0, 0], me % 4]).astype(i32)

    q_blocks = call(pack_queries_kernel, shape((32, SLOT_PAD, BLOCK), bf16), n_in=1)(fresh_qkv[0, :, 0])
    q_all = lax.all_to_all(q_blocks, SEQ, 0, 0, tiled=True)

    kv_new = jnp.swapaxes(fresh_qkv[0, :, 1:3], 0, 1)
    keep, send = call(
        pack_cache_kernel,
        [shape((4, 2, tokens, BLOCK), bf16)] * 2,
        scratch=[pltpu.VMEM((2, tokens, width), bf16)],
        n_in=4,
        smem=(0,),
    )(info, kv_cache[0], kv_new, chosen)
    swap = [(position(z, x, c), position(z, x, 1 - c)) for z in range(4) for x in range(4) for c in range(2)]
    first = lax.ppermute(send, SEQ, swap)
    others = [lax.ppermute(jnp.stack([keep[k], first[k]]), SEQ, ring_pairs(k)) for k in (1, 2, 3)]

    parts = call(
        attention_kernel,
        shape((32, SLOT_PAD, BLOCK), bf16),
        scratch=[pltpu.VMEM((8 * tokens, BLOCK), bf16), pltpu.VMEM((HEADS_HERE, HEAD_DIM, 8 * tokens), bf16)],
        n_in=6,
        limit=24,
    )(q_all, keep, first, *others)
    parts = lax.all_to_all(parts, SEQ, 0, 0, tiled=True)

    hidden, normed = call(
        combine_kernel,
        [shape((SLOT_PAD, width), f32), shape((SLOT_PAD, width), bf16)],
        scratch=[pltpu.VMEM((128, 128), f32), pltpu.VMEM((128, 128), f32)],
        n_in=4,
        smem=(0,),
    )(info, parts, rows_in, modulation)

    normed_all = lax.all_gather(normed, "y", axis=0, tiled=True)
    terms = feed_forward(normed_all, w_up, b_up[None], w_down)
    terms = lax.all_to_all(terms.reshape(4, SLOT_PAD, width), "y", 0, 0, tiled=True)
    return call(finish_kernel, shape((1, slots, width), bf16), n_in=5, smem=(0,))(
        info, terms, hidden, modulation, b_down[None]
    )


def solution(mesh):
    whole = jax.sharding.Mesh(mesh.devices.reshape(4, 4, 4, 2), ("y", "z", "x", "core"))
    placed = (
        P("y", SEQ, None),
        P("y", SEQ, None, None),
        P("y", SEQ, None, None),
        P("y", SEQ),
        P("y", SEQ),
        P("y", None, None),
        P(None, "y"),
        P("y"),
        P("y", None),
        P(),
    )
    return jax.shard_map(body, mesh=whole, in_specs=placed, out_specs=P("y", SEQ, None), check_vma=False)
```

```python
import jax
import jax.numpy as jnp
from jax import lax
from jax.experimental import pallas as pl
from jax.experimental.pallas import tpu as pltpu
from jax.sharding import PartitionSpec as P

HEAD_DIM = 128
HEADS_HERE = 3
BLOCK = HEADS_HERE * HEAD_DIM
SLOT_PAD = 32
LOG2E = 1.4426950408889634
EPS = 1e-06
SEQ = ("z", "x", "core")
bf16 = jnp.bfloat16
f32 = jnp.float32
i32 = jnp.int32
MB = 1 << 20


def call(kernel, out_shape, scratch=(), limit=16, smem=(), hbm=(), n_in=None, us=1.0):
    def space(i):
        return pltpu.SMEM if i in smem else pltpu.HBM if i in hbm else pltpu.VMEM

    return pl.pallas_call(
        kernel,
        out_shape=out_shape,
        in_specs=[pl.BlockSpec(memory_space=space(i)) for i in range(n_in)],
        scratch_shapes=list(scratch),
        compiler_params=pltpu.CompilerParams(vmem_limit_bytes=limit * MB),
        cost_estimate=pl.CostEstimate(flops=0, transcendentals=0, bytes_accessed=int(us * 3.3e6)),
    )


def fetch(pairs, sems):
    copies = [pltpu.make_async_copy(src, dst, sems.at[i]) for i, (src, dst) in enumerate(pairs)]
    for copy in copies:
        copy.start()
    for copy in copies:
        copy.wait()


def pack_queries_kernel(fresh_ref, out_ref, q_ref, sems):
    rows = q_ref.shape[0]
    fetch([(fresh_ref.at[0], q_ref)], sems)
    for dest in range(32):
        z, x, core = dest // 8, dest // 2 % 4, dest % 2
        group = x if core == 0 else 4 + z
        out_ref[dest, :rows, :] = q_ref[:, group * BLOCK : (group + 1) * BLOCK]
        out_ref[dest, rows:, :] = jnp.zeros((SLOT_PAD - rows, BLOCK), bf16)


def pack_cache_kernel(
    info_ref, kv_hbm, fresh_ref, chosen_ref, after_ref, keep_ref, send_ref, kv_ref, kv_new_ref, patched, sems
):
    fetch([(kv_hbm, kv_ref), (fresh_ref.at[1:3], kv_new_ref)], sems)
    tokens = kv_ref.shape[0]
    slots = kv_new_ref.shape[1]
    core, ring_x, ring_z, count = info_ref[0], info_ref[1], info_ref[2], info_ref[3]
    token_id = lax.broadcasted_iota(i32, (tokens, slots), 0)
    slot_id = lax.broadcasted_iota(i32, (tokens, slots), 1)
    hit = (token_id == chosen_ref[...]) & (slot_id < count)
    hot = jnp.where(hit, 1.0, 0.0)
    taken = jnp.sum(hot, axis=1, keepdims=True) > 0.5
    hot = hot.astype(bf16)
    old = jnp.swapaxes(kv_ref[...], 0, 1)
    for which in range(2):
        new = jnp.dot(hot, kv_new_ref[which], preferred_element_type=f32)
        patched[which] = jnp.where(taken, new, old[which].astype(f32)).astype(bf16)
    half = 4 * BLOCK
    for k in range(4):
        mine = lax.rem(jnp.where(core == 0, ring_x, ring_z) + k, 4)
        other = lax.rem(jnp.where(core == 0, ring_z, ring_x) + k, 4)
        at_mine = pl.multiple_of(core * half + mine * BLOCK, BLOCK)
        at_other = pl.multiple_of((1 - core) * half + other * BLOCK, BLOCK)
        for which in range(2):
            keep_ref[k, which] = patched[which, :, pl.ds(at_mine, BLOCK)]
            send_ref[k, which] = patched[which, :, pl.ds(at_other, BLOCK)]


def stack_kernel(keep_ref, first_ref, *out_refs):
    for k, out_ref in enumerate(out_refs):
        out_ref[0] = keep_ref[k]
        out_ref[1] = first_ref[k]


def attention_kernel(q_ref, r0_ref, r1_ref, r2_ref, r3_ref, out_ref, keys, values_t):
    sources = [ref.at[core] for ref in (r0_ref, r1_ref, r2_ref, r3_ref) for core in range(2)]
    for i, ref in enumerate(sources):
        keys[i * 128 : (i + 1) * 128, :] = ref[0]
        for h in range(HEADS_HERE):
            cols = slice(h * HEAD_DIM, (h + 1) * HEAD_DIM)
            values_t[h, :, i * 128 : (i + 1) * 128] = ref[1, :, cols].T
    scale = LOG2E * HEAD_DIM**-0.5
    tile = 1024
    blocks = tile // SLOT_PAD

    def step(t, _):
        q_all = q_ref[pl.ds(t * blocks, blocks)].reshape(tile, BLOCK)
        for h in range(HEADS_HERE):
            cols = slice(h * HEAD_DIM, (h + 1) * HEAD_DIM)
            scores = lax.dot_general(
                keys[:, cols], q_all[:, cols], (((1,), (1,)), ((), ())), preferred_element_type=f32
            )
            top = jnp.max(scores, axis=0, keepdims=True)
            weights = jnp.exp2((scores - top) * scale)
            mass = jnp.sum(weights, axis=0, keepdims=True)
            mixed = jnp.dot(values_t[h], weights.astype(bf16), preferred_element_type=f32)
            mixed = mixed * (1.0 / mass)
            level = top * scale + jnp.log2(mass)
            p0 = level.astype(bf16).astype(f32)
            rest = level - p0
            p1 = rest.astype(bf16).astype(f32)
            p2 = rest - p1
            for g in range(tile // 128):
                lanes = slice(g * 128, (g + 1) * 128)
                turned = mixed[:, lanes].T
                row = lax.broadcasted_iota(i32, (128, HEAD_DIM), 0) % SLOT_PAD
                turned = jnp.where(row == 28, p0[:, lanes], turned)
                turned = jnp.where(row == 29, p1[:, lanes], turned)
                turned = jnp.where(row == 30, p2[:, lanes], turned)
                out_ref[pl.ds(t * blocks + g * 4, 4), :, cols] = turned.astype(bf16).reshape(
                    4, SLOT_PAD, HEAD_DIM
                )
        return 0

    lax.fori_loop(0, q_ref.shape[0] // blocks, step, 0)


def combine_kernel(
    info_ref, parts_ref, rows_hbm, mod_hbm, hidden_ref, normed_ref, levels, turned, rows_ref, mod_ref, sems
):
    slots = rows_ref.shape[1]
    copies = [
        pltpu.make_async_copy(rows_hbm, rows_ref, sems.at[0]),
        pltpu.make_async_copy(mod_hbm, mod_ref, sems.at[1]),
    ]
    for copy in copies:
        copy.start()
    heads = 24

    def source(part, group):
        return part * 8 + group * 2 if group < 4 else (group - 4) * 8 + part * 2 + 1

    for part in range(4):
        for group in range(8):
            tail = parts_ref[source(part, group), 24:32, :].astype(f32)
            level = tail[4:5] + tail[5:6] + tail[6:7]
            for h in range(HEADS_HERE):
                at = part * heads + group * HEADS_HERE + h
                levels[at : at + 1, :] = level[:, h * HEAD_DIM : (h + 1) * HEAD_DIM]
    pieces = [levels[p * heads : (p + 1) * heads, :] for p in range(4)]
    top = jnp.maximum(jnp.maximum(pieces[0], pieces[1]), jnp.maximum(pieces[2], pieces[3]))
    weights = [jnp.exp2(piece - top) for piece in pieces]
    total = 1.0 / (weights[0] + weights[1] + weights[2] + weights[3])
    for p in range(4):
        levels[p * heads : (p + 1) * heads, :] = weights[p] * total
    levels[4 * heads :, :] = jnp.zeros((128 - 4 * heads, 128), f32)
    turned[...] = levels[...].T
    mine = turned[pl.ds(pl.multiple_of(info_ref[4] * SLOT_PAD, SLOT_PAD), SLOT_PAD), :]
    for copy in copies:
        copy.wait()
    shifts = mod_ref[0].astype(f32)
    for group in range(8):
        for h in range(HEADS_HERE):
            head = group * HEADS_HERE + h
            acc = jnp.zeros((SLOT_PAD, HEAD_DIM), f32)
            for part in range(4):
                column = part * heads + head
                block = parts_ref[source(part, group), :, h * HEAD_DIM : (h + 1) * HEAD_DIM]
                acc = acc + mine[:, column : column + 1] * block.astype(f32)
            cols = slice(head * HEAD_DIM, (head + 1) * HEAD_DIM)
            attended = acc[:slots] * shifts[2:3, cols]
            hidden_ref[:slots, cols] = rows_ref[0, :, cols].astype(f32) + attended
    hidden_ref[slots:, :] = jnp.zeros((SLOT_PAD - slots, hidden_ref.shape[1]), f32)
    hidden = hidden_ref[...]
    center = hidden - jnp.mean(hidden, axis=1, keepdims=True)
    spread = jnp.mean(center * center, axis=1, keepdims=True)
    normed = center * lax.rsqrt(spread + EPS) * (1.0 + shifts[1:2]) + shifts[0:1]
    normed_ref[...] = normed.astype(bf16)


def load_kernel(after_ref, weight, out_ref, sems):
    fetch([(weight, out_ref)], sems)


def load(after, weight, limit):
    return call(
        load_kernel,
        jax.ShapeDtypeStruct(weight.shape, bf16),
        scratch=[pltpu.SemaphoreType.DMA((1,))],
        n_in=2,
        hbm=(0, 1),
        limit=limit,
        us=3.6,
    )(after, weight)


def feed_kernel(r0_ref, r1_ref, r2_ref, r3_ref, up_ref, b_up_ref, down_ref, o0, o1, o2, o3, rows_ref, active):
    chunk = 512
    for i, ref in enumerate((r0_ref, r1_ref, r2_ref, r3_ref)):
        rows_ref[i * SLOT_PAD : (i + 1) * SLOT_PAD, :] = ref[...]
    rows = rows_ref[...]
    for start in range(0, up_ref.shape[1], chunk):
        cols = slice(start, start + chunk)
        lifted = jnp.dot(rows, up_ref[:, cols], preferred_element_type=f32)
        lifted = lifted + b_up_ref[:, cols].astype(f32)
        active[:, cols] = jax.nn.gelu(lifted, approximate=True).astype(bf16)
    for start in range(0, down_ref.shape[1], chunk):
        cols = slice(start, start + chunk)
        terms = jnp.dot(active[...], down_ref[:, cols], preferred_element_type=f32)
        for i, out_ref in enumerate((o0, o1, o2, o3)):
            out_ref[:, cols] = terms[i * SLOT_PAD : (i + 1) * SLOT_PAD].astype(bf16)


def finish_kernel(info_ref, t0_ref, t1_ref, t2_ref, t3_ref, hidden_ref, mod_ref, b_down_ref, out_ref):
    slots = out_ref.shape[1]
    total = t0_ref[...].astype(f32)
    for ref in (t1_ref, t2_ref, t3_ref):
        total = total + ref[...].astype(f32)
    feed_out = total[:slots] + b_down_ref[...].astype(f32)
    result = hidden_ref[:slots] + mod_ref[0, 3:4].astype(f32) * feed_out
    live = lax.broadcasted_iota(i32, result.shape, 0) < info_ref[3]
    out_ref[0] = jnp.where(live, result, 0.0).astype(bf16)


def position(z, x, core):
    return (z % 4) * 8 + (x % 4) * 2 + core


def ring_pairs(k):
    return [
        (position(z, x, c), position(z, x + k, 0) if c == 0 else position(z + k, x, 1))
        for z in range(4)
        for x in range(4)
        for c in range(2)
    ]


def turn(k):
    return [(y, (y + k) % 4) for y in range(4)]


def body(rows_in, fresh_qkv, kv_cache, chosen, counts, modulation, w_up, b_up, w_down, b_down):
    shape = jax.ShapeDtypeStruct
    slots, width = rows_in.shape[1], rows_in.shape[2]
    tokens = kv_cache.shape[1]
    core, ring_x, ring_z = (lax.axis_index(a) for a in ("core", "x", "z"))
    me = ring_z * 8 + ring_x * 2 + core
    info = jnp.stack([core, ring_x, ring_z, counts[0, 0], me % 4]).astype(i32)

    fresh = jnp.swapaxes(fresh_qkv[0], 0, 1)
    q_blocks = call(
        pack_queries_kernel,
        shape((32, SLOT_PAD, BLOCK), bf16),
        scratch=[pltpu.VMEM((slots, width), bf16), pltpu.SemaphoreType.DMA((1,))],
        n_in=1,
        hbm=(0,),
        limit=61,
    )(fresh)
    q_all = lax.all_to_all(q_blocks, SEQ, 0, 0, tiled=True)

    keep, send = call(
        pack_cache_kernel,
        [shape((4, 2, tokens, BLOCK), bf16)] * 2,
        scratch=[
            pltpu.VMEM((tokens, 2, width), bf16),
            pltpu.VMEM((2, slots, width), bf16),
            pltpu.VMEM((2, tokens, width), bf16),
            pltpu.SemaphoreType.DMA((2,)),
        ],
        n_in=5,
        smem=(0,),
        hbm=(1, 2, 4),
        limit=61,
        us=3.0,
    )(info, kv_cache[0], fresh, chosen, q_blocks)
    swap = [(position(z, x, c), position(z, x, 1 - c)) for z in range(4) for x in range(4) for c in range(2)]
    first = lax.ppermute(send, SEQ, swap)
    stacked = call(stack_kernel, [shape((2, 2, tokens, BLOCK), bf16)] * 4, n_in=2)(keep, first)
    others = [lax.ppermute(stacked[k], SEQ, ring_pairs(k)) for k in (1, 2, 3)]

    partial = call(
        attention_kernel,
        shape((32, SLOT_PAD, BLOCK), bf16),
        scratch=[pltpu.VMEM((8 * tokens, BLOCK), bf16), pltpu.VMEM((HEADS_HERE, HEAD_DIM, 8 * tokens), bf16)],
        n_in=5,
        limit=24,
        us=6.5,
    )(q_all, stacked[0], *others)
    parts = lax.all_to_all(partial, SEQ, 0, 0, tiled=True)
    hidden, normed = call(
        combine_kernel,
        [shape((SLOT_PAD, width), f32), shape((SLOT_PAD, width), bf16)],
        scratch=[
            pltpu.VMEM((128, 128), f32),
            pltpu.VMEM((128, 128), f32),
            pltpu.VMEM(rows_in.shape, bf16),
            pltpu.VMEM(modulation.shape, bf16),
            pltpu.SemaphoreType.DMA((2,)),
        ],
        n_in=4,
        smem=(0,),
        hbm=(2, 3),
        limit=60,
        us=1.6,
    )(info, parts, rows_in, modulation)

    visits = [lax.ppermute(normed, "y", turn(k)) for k in (1, 2, 3)]
    up = load(normed, w_up, 44)
    down = load(normed, w_down, 36)
    terms = call(
        feed_kernel,
        [shape((SLOT_PAD, width), bf16)] * 4,
        scratch=[pltpu.VMEM((4 * SLOT_PAD, width), bf16), pltpu.VMEM((4 * SLOT_PAD, w_up.shape[1]), bf16)],
        n_in=7,
        us=3.7,
    )(normed, *visits, up, b_up[None], down)
    back = [lax.ppermute(terms[k], "y", turn(-k)) for k in (1, 2, 3)]
    return call(finish_kernel, shape((1, slots, width), bf16), n_in=8, smem=(0,), us=1.4)(
        info, terms[0], *back, hidden, modulation, b_down[None]
    )


def solution(mesh):
    whole = jax.sharding.Mesh(mesh.devices.reshape(4, 4, 4, 2), ("y", "z", "x", "core"))
    placed = (
        P("y", SEQ, None),
        P("y", SEQ, None, None),
        P("y", SEQ, None, None),
        P("y", SEQ),
        P("y", SEQ),
        P("y", None, None),
        P(None, "y"),
        P("y"),
        P("y", None),
        P(),
    )
    return jax.shard_map(body, mesh=whole, in_specs=placed, out_specs=P("y", SEQ, None), check_vma=False)
```

```python
import jax
import jax.numpy as jnp
from jax import lax
from jax.experimental import pallas as pl
from jax.experimental.pallas import tpu as pltpu
from jax.sharding import PartitionSpec as P

HEAD_DIM = 128
HEADS_HERE = 3
BLOCK = HEADS_HERE * HEAD_DIM
SLOT_PAD = 32
LOG2E = 1.4426950408889634
EPS = 1e-06
SEQ = ("z", "x", "core")
bf16 = jnp.bfloat16
f32 = jnp.float32
i32 = jnp.int32
MB = 1 << 20


def call(kernel, out_shape, scratch=(), limit=16, smem=(), hbm=(), n_in=None, us=1.0):
    def space(i):
        return pltpu.SMEM if i in smem else pltpu.HBM if i in hbm else pltpu.VMEM

    return pl.pallas_call(
        kernel,
        out_shape=out_shape,
        in_specs=[pl.BlockSpec(memory_space=space(i)) for i in range(n_in)],
        scratch_shapes=list(scratch),
        compiler_params=pltpu.CompilerParams(vmem_limit_bytes=limit * MB),
        cost_estimate=pl.CostEstimate(flops=0, transcendentals=0, bytes_accessed=int(us * 3.3e6)),
    )


def fetch(pairs, sems):
    copies = [pltpu.make_async_copy(src, dst, sems.at[i]) for i, (src, dst) in enumerate(pairs)]
    for copy in copies:
        copy.start()
    for copy in copies:
        copy.wait()


def pack_queries_kernel(fresh_ref, out_ref, q_ref, sems):
    rows = q_ref.shape[0]
    fetch([(fresh_ref.at[0], q_ref)], sems)
    for dest in range(32):
        z, x, core = dest // 8, dest // 2 % 4, dest % 2
        group = x if core == 0 else 4 + z
        out_ref[dest, :rows, :] = q_ref[:, group * BLOCK : (group + 1) * BLOCK]
        out_ref[dest, rows:, :] = jnp.zeros((SLOT_PAD - rows, BLOCK), bf16)


def pack_cache_kernel(
    count_ref, kv_ref, fresh_ref, chosen_ref, keep_ref, send_ref, patched
):
    tokens = kv_ref.shape[0]
    slots = fresh_ref.shape[1]
    core, ring_x, ring_z = (lax.axis_index(a) for a in ("core", "x", "z"))
    count = count_ref[0, 0]
    token_id = lax.broadcasted_iota(i32, (tokens, slots), 0)
    slot_id = lax.broadcasted_iota(i32, (tokens, slots), 1)
    hit = (token_id == chosen_ref[...]) & (slot_id < count)
    hot = jnp.where(hit, 1.0, 0.0)
    taken = jnp.sum(hot, axis=1, keepdims=True) > 0.5
    hot = hot.astype(bf16)
    old = jnp.swapaxes(kv_ref[...], 0, 1)
    for which in range(2):
        new = jnp.dot(hot, fresh_ref[1 + which], preferred_element_type=f32)
        patched[which] = jnp.where(taken, new, old[which].astype(f32)).astype(bf16)
    half = 4 * BLOCK
    for k in range(4):
        mine = lax.rem(jnp.where(core == 0, ring_x, ring_z) + k, 4)
        other = lax.rem(jnp.where(core == 0, ring_z, ring_x) + k, 4)
        at_mine = pl.multiple_of(core * half + mine * BLOCK, BLOCK)
        at_other = pl.multiple_of((1 - core) * half + other * BLOCK, BLOCK)
        for which in range(2):
            keep_ref[k, which] = patched[which, :, pl.ds(at_mine, BLOCK)]
            send_ref[k, which] = patched[which, :, pl.ds(at_other, BLOCK)]


def stack_kernel(keep_ref, first_ref, *out_refs):
    for k, out_ref in enumerate(out_refs):
        out_ref[0] = keep_ref[k]
        out_ref[1] = first_ref[k]


def attention_kernel(q_ref, r0_ref, r1_ref, r2_ref, r3_ref, out_ref, keys, values_t):
    sources = [ref.at[core] for ref in (r0_ref, r1_ref, r2_ref, r3_ref) for core in range(2)]
    for i, ref in enumerate(sources):
        keys[i * 128 : (i + 1) * 128, :] = ref[0]
        for h in range(HEADS_HERE):
            cols = slice(h * HEAD_DIM, (h + 1) * HEAD_DIM)
            values_t[h, :, i * 128 : (i + 1) * 128] = ref[1, :, cols].T
    scale = LOG2E * HEAD_DIM**-0.5
    tile = 1024
    blocks = tile // SLOT_PAD

    def step(t, _):
        q_all = q_ref[pl.ds(t * blocks, blocks)].reshape(tile, BLOCK)
        for h in range(HEADS_HERE):
            cols = slice(h * HEAD_DIM, (h + 1) * HEAD_DIM)
            scores = lax.dot_general(
                keys[:, cols], q_all[:, cols], (((1,), (1,)), ((), ())), preferred_element_type=f32
            )
            top = jnp.max(scores, axis=0, keepdims=True)
            weights = jnp.exp2((scores - top) * scale)
            mass = jnp.sum(weights, axis=0, keepdims=True)
            mixed = jnp.dot(values_t[h], weights.astype(bf16), preferred_element_type=f32)
            mixed = mixed * (1.0 / mass)
            level = top * scale + jnp.log2(mass)
            p0 = level.astype(bf16).astype(f32)
            rest = level - p0
            p1 = rest.astype(bf16).astype(f32)
            p2 = rest - p1
            for g in range(tile // 128):
                lanes = slice(g * 128, (g + 1) * 128)
                turned = mixed[:, lanes].T
                row = lax.broadcasted_iota(i32, (128, HEAD_DIM), 0) % SLOT_PAD
                turned = jnp.where(row == 28, p0[:, lanes], turned)
                turned = jnp.where(row == 29, p1[:, lanes], turned)
                turned = jnp.where(row == 30, p2[:, lanes], turned)
                out_ref[pl.ds(t * blocks + g * 4, 4), :, cols] = turned.astype(bf16).reshape(
                    4, SLOT_PAD, HEAD_DIM
                )
        return 0

    lax.fori_loop(0, q_ref.shape[0] // blocks, step, 0)


def combine_kernel(parts_ref, rows_ref, mod_ref, hidden_ref, normed_ref, mark_ref, levels, turned):
    slots = rows_ref.shape[1]
    place = 2 * lax.rem(lax.axis_index("x"), 2) + lax.axis_index("core")
    heads = 24

    def source(part, group):
        return part * 8 + group * 2 if group < 4 else (group - 4) * 8 + part * 2 + 1

    for part in range(4):
        for group in range(8):
            tail = parts_ref[source(part, group), 24:32, :].astype(f32)
            level = tail[4:5] + tail[5:6] + tail[6:7]
            for h in range(HEADS_HERE):
                at = part * heads + group * HEADS_HERE + h
                levels[at : at + 1, :] = level[:, h * HEAD_DIM : (h + 1) * HEAD_DIM]
    pieces = [levels[p * heads : (p + 1) * heads, :] for p in range(4)]
    top = jnp.maximum(jnp.maximum(pieces[0], pieces[1]), jnp.maximum(pieces[2], pieces[3]))
    weights = [jnp.exp2(piece - top) for piece in pieces]
    total = 1.0 / (weights[0] + weights[1] + weights[2] + weights[3])
    for p in range(4):
        levels[p * heads : (p + 1) * heads, :] = weights[p] * total
    levels[4 * heads :, :] = jnp.zeros((128 - 4 * heads, 128), f32)
    turned[...] = levels[...].T
    mine = turned[pl.ds(pl.multiple_of(place * SLOT_PAD, SLOT_PAD), SLOT_PAD), :]
    shifts = mod_ref[0].astype(f32)
    for group in range(8):
        for h in range(HEADS_HERE):
            head = group * HEADS_HERE + h
            acc = jnp.zeros((SLOT_PAD, HEAD_DIM), f32)
            for part in range(4):
                column = part * heads + head
                block = parts_ref[source(part, group), :, h * HEAD_DIM : (h + 1) * HEAD_DIM]
                acc = acc + mine[:, column : column + 1] * block.astype(f32)
            cols = slice(head * HEAD_DIM, (head + 1) * HEAD_DIM)
            attended = acc[:slots] * shifts[2:3, cols]
            hidden_ref[:slots, cols] = rows_ref[0, :, cols].astype(f32) + attended
    hidden_ref[slots:, :] = jnp.zeros((SLOT_PAD - slots, hidden_ref.shape[1]), f32)
    hidden = hidden_ref[...]
    center = hidden - jnp.mean(hidden, axis=1, keepdims=True)
    spread = jnp.mean(center * center, axis=1, keepdims=True)
    normed = center * lax.rsqrt(spread + EPS) * (1.0 + shifts[1:2]) + shifts[0:1]
    normed_ref[...] = normed.astype(bf16)
    mark_ref[...] = jnp.zeros(mark_ref.shape, bf16)


def load_kernel(after_ref, *refs):
    count = len(refs) // 2
    fetch(list(zip(refs[:count], refs[count : 2 * count])), refs[2 * count])


def load(after, arrays, limit):
    return call(
        load_kernel,
        [jax.ShapeDtypeStruct(v.shape, bf16) for v in arrays],
        scratch=[pltpu.SemaphoreType.DMA((len(arrays),))],
        n_in=1 + len(arrays),
        hbm=range(1 + len(arrays)),
        limit=limit,
        us=3.6,
    )(after, *arrays)


def feed_kernel(r0_ref, r1_ref, r2_ref, r3_ref, up_ref, b_up_ref, down_ref, o0, o1, o2, o3, rows_ref, active):
    chunk = 512
    for i, ref in enumerate((r0_ref, r1_ref, r2_ref, r3_ref)):
        rows_ref[i * SLOT_PAD : (i + 1) * SLOT_PAD, :] = ref[...]
    rows = rows_ref[...]
    for start in range(0, up_ref.shape[1], chunk):
        cols = slice(start, start + chunk)
        lifted = jnp.dot(rows, up_ref[:, cols], preferred_element_type=f32)
        lifted = lifted + b_up_ref[:, cols].astype(f32)
        active[:, cols] = jax.nn.gelu(lifted, approximate=True).astype(bf16)
    for start in range(0, down_ref.shape[1], chunk):
        cols = slice(start, start + chunk)
        terms = jnp.dot(active[...], down_ref[:, cols], preferred_element_type=f32)
        for i, out_ref in enumerate((o0, o1, o2, o3)):
            out_ref[:, cols] = terms[i * SLOT_PAD : (i + 1) * SLOT_PAD].astype(bf16)


def finish_kernel(count_ref, t0_ref, t1_ref, t2_ref, t3_ref, hidden_ref, mod_ref, b_down_ref, out_ref):
    slots = out_ref.shape[1]
    total = t0_ref[...].astype(f32)
    for ref in (t1_ref, t2_ref, t3_ref):
        total = total + ref[...].astype(f32)
    feed_out = total[:slots] + b_down_ref[...].astype(f32)
    result = hidden_ref[:slots] + mod_ref[0, 3:4].astype(f32) * feed_out
    live = lax.broadcasted_iota(i32, result.shape, 0) < count_ref[0, 0]
    out_ref[0] = jnp.where(live, result, 0.0).astype(bf16)


def position(z, x, core):
    return (z % 4) * 8 + (x % 4) * 2 + core


def ring_pairs(k):
    return [
        (position(z, x, c), position(z, x + k, 0) if c == 0 else position(z + k, x, 1))
        for z in range(4)
        for x in range(4)
        for c in range(2)
    ]


def turn(k):
    return [(y, (y + k) % 4) for y in range(4)]


def body(rows_in, fresh_qkv, kv_cache, chosen, counts, modulation, w_up, b_up, w_down, b_down):
    shape = jax.ShapeDtypeStruct
    slots, width = rows_in.shape[1], rows_in.shape[2]
    tokens = kv_cache.shape[1]
    fresh = jnp.swapaxes(fresh_qkv[0], 0, 1)
    q_blocks = call(
        pack_queries_kernel,
        shape((32, SLOT_PAD, BLOCK), bf16),
        scratch=[pltpu.VMEM((slots, width), bf16), pltpu.SemaphoreType.DMA((1,))],
        n_in=1,
        hbm=(0,),
        limit=61,
    )(fresh)
    q_all = lax.all_to_all(q_blocks, SEQ, 0, 0, tiled=True)

    keep, send = call(
        pack_cache_kernel,
        [shape((4, 2, tokens, BLOCK), bf16)] * 2,
        scratch=[pltpu.VMEM((2, tokens, width), bf16)],
        n_in=4,
        smem=(0,),
        us=3.0,
    )(counts, kv_cache[0], fresh, chosen)
    swap = [(position(z, x, c), position(z, x, 1 - c)) for z in range(4) for x in range(4) for c in range(2)]
    first = lax.ppermute(send, SEQ, swap)
    stacked = call(stack_kernel, [shape((2, 2, tokens, BLOCK), bf16)] * 4, n_in=2, us=0.5)(keep, first)
    others = [lax.ppermute(stacked[k], SEQ, ring_pairs(k)) for k in (1, 2, 3)]

    partial = call(
        attention_kernel,
        shape((32, SLOT_PAD, BLOCK), bf16),
        scratch=[pltpu.VMEM((8 * tokens, BLOCK), bf16), pltpu.VMEM((HEADS_HERE, HEAD_DIM, 8 * tokens), bf16)],
        n_in=5,
        limit=24,
        us=6.5,
    )(q_all, stacked[0], *others)
    parts = lax.all_to_all(partial, SEQ, 0, 0, tiled=True)
    rows, mod = load(partial, [rows_in, modulation], 16)
    hidden, normed, mark = call(
        combine_kernel,
        [shape((SLOT_PAD, width), f32), shape((SLOT_PAD, width), bf16), shape((16, 128), bf16)],
        scratch=[pltpu.VMEM((128, 128), f32), pltpu.VMEM((128, 128), f32)],
        n_in=3,
        us=1.6,
    )(parts, rows, mod)

    visits = [lax.ppermute(normed, "y", turn(k)) for k in (1, 2, 3)]
    up, down = load(mark, [w_up, w_down], 34)
    terms = call(
        feed_kernel,
        [shape((SLOT_PAD, width), bf16)] * 4,
        scratch=[pltpu.VMEM((4 * SLOT_PAD, width), bf16), pltpu.VMEM((4 * SLOT_PAD, w_up.shape[1]), bf16)],
        n_in=7,
        us=3.7,
    )(normed, *visits, up, b_up[None], down)
    back = [lax.ppermute(terms[k], "y", turn(-k)) for k in (1, 2, 3)]
    return call(finish_kernel, shape((1, slots, width), bf16), n_in=8, smem=(0,), us=1.4)(
        counts, terms[0], *back, hidden, modulation, b_down[None]
    )


def solution(mesh):
    whole = jax.sharding.Mesh(mesh.devices.reshape(4, 4, 4, 2), ("y", "z", "x", "core"))
    placed = (
        P("y", SEQ, None),
        P("y", SEQ, None, None),
        P("y", SEQ, None, None),
        P("y", SEQ),
        P("y", SEQ),
        P("y", None, None),
        P(None, "y"),
        P("y"),
        P("y", None),
        P(),
    )
    return jax.shard_map(body, mesh=whole, in_specs=placed, out_specs=P("y", SEQ, None), check_vma=False)
```

```python
import jax
import jax.numpy as jnp
from jax import lax
from jax.experimental import pallas as pl
from jax.experimental.pallas import tpu as pltpu
from jax.sharding import PartitionSpec as P

HEAD_DIM = 128
HEADS_HERE = 3
BLOCK = HEADS_HERE * HEAD_DIM
SLOT_PAD = 32
LOG2E = 1.4426950408889634
EPS = 1e-06
SEQ = ("z", "x", "core")
bf16 = jnp.bfloat16
f32 = jnp.float32
i32 = jnp.int32
MB = 1 << 20


def call(kernel, out_shape, scratch=(), limit=16, smem=(), hbm=(), n_in=None, us=1.0):
    def space(i):
        return pltpu.SMEM if i in smem else pltpu.HBM if i in hbm else pltpu.VMEM

    return pl.pallas_call(
        kernel,
        out_shape=out_shape,
        in_specs=[pl.BlockSpec(memory_space=space(i)) for i in range(n_in)],
        scratch_shapes=list(scratch),
        compiler_params=pltpu.CompilerParams(vmem_limit_bytes=limit * MB),
        cost_estimate=pl.CostEstimate(flops=0, transcendentals=0, bytes_accessed=int(us * 3.3e6)),
    )


def fetch(pairs, sems):
    copies = [pltpu.make_async_copy(src, dst, sems.at[i]) for i, (src, dst) in enumerate(pairs)]
    for copy in copies:
        copy.start()
    for copy in copies:
        copy.wait()


def pack_kernel(
    count_ref, kv_hbm, fresh_hbm, chosen_hbm, q_hbm, keep_hbm, send_hbm,
    kv_ref, fresh_ref, chosen_ref, patched, q_out, in_sems, out_sems,
):
    sources = [
        (fresh_hbm.at[0], fresh_ref.at[0]),
        (kv_hbm, kv_ref),
        (fresh_hbm.at[1:3], fresh_ref.at[1:3]),
        (chosen_hbm, chosen_ref),
    ]
    copies = [pltpu.make_async_copy(src, dst, in_sems.at[i]) for i, (src, dst) in enumerate(sources)]
    for copy in copies:
        copy.start()
    tokens = kv_ref.shape[0]
    slots = fresh_ref.shape[1]
    copies[0].wait()
    for dest in range(32):
        z, x, core = dest // 8, dest // 2 % 4, dest % 2
        group = x if core == 0 else 4 + z
        q_out[dest, :slots, :] = fresh_ref[0, :, group * BLOCK : (group + 1) * BLOCK]
        q_out[dest, slots:, :] = jnp.zeros((SLOT_PAD - slots, BLOCK), bf16)
    outs = [pltpu.make_async_copy(q_out, q_hbm, out_sems.at[0])]
    outs[0].start()

    core, ring_x, ring_z = (lax.axis_index(a) for a in ("core", "x", "z"))
    count = count_ref[0, 0]
    for copy in copies[1:]:
        copy.wait()
    token_id = lax.broadcasted_iota(i32, (tokens, slots), 0)
    slot_id = lax.broadcasted_iota(i32, (tokens, slots), 1)
    hit = (token_id == chosen_ref[...]) & (slot_id < count)
    hot = jnp.where(hit, 1.0, 0.0)
    taken = jnp.sum(hot, axis=1, keepdims=True) > 0.5
    hot = hot.astype(bf16)
    old = jnp.swapaxes(kv_ref[...], 0, 1)
    half = 4 * BLOCK
    for which in range(2):
        new = jnp.dot(hot, fresh_ref[1 + which], preferred_element_type=f32)
        patched[which] = jnp.where(taken, new, old[which].astype(f32)).astype(bf16)
        for k in range(4):
            mine = lax.rem(jnp.where(core == 0, ring_x, ring_z) + k, 4)
            other = lax.rem(jnp.where(core == 0, ring_z, ring_x) + k, 4)
            at_mine = pl.multiple_of(core * half + mine * BLOCK, BLOCK)
            at_other = pl.multiple_of((1 - core) * half + other * BLOCK, BLOCK)
            for at, target in ((at_other, send_hbm), (at_mine, keep_hbm)):
                copy = pltpu.make_async_copy(
                    patched.at[which, :, pl.ds(at, BLOCK)], target.at[k, which], out_sems.at[len(outs)]
                )
                copy.start()
                outs.append(copy)
    for copy in outs:
        copy.wait()


def stack_kernel(keep_ref, first_ref, *out_refs):
    for k, out_ref in enumerate(out_refs):
        out_ref[0] = keep_ref[k]
        out_ref[1] = first_ref[k]


def attention_kernel(q_ref, r0_ref, r1_ref, r2_ref, r3_ref, out_ref, keys, values_t):
    sources = [ref.at[core] for ref in (r0_ref, r1_ref, r2_ref, r3_ref) for core in range(2)]
    for i, ref in enumerate(sources):
        keys[i * 128 : (i + 1) * 128, :] = ref[0]
        for h in range(HEADS_HERE):
            cols = slice(h * HEAD_DIM, (h + 1) * HEAD_DIM)
            values_t[h, :, i * 128 : (i + 1) * 128] = ref[1, :, cols].T
    scale = LOG2E * HEAD_DIM**-0.5
    tile = 1024
    blocks = tile // SLOT_PAD

    def step(t, _):
        q_all = q_ref[pl.ds(t * blocks, blocks)].reshape(tile, BLOCK)
        for h in range(HEADS_HERE):
            cols = slice(h * HEAD_DIM, (h + 1) * HEAD_DIM)
            scores = lax.dot_general(
                keys[:, cols], q_all[:, cols], (((1,), (1,)), ((), ())), preferred_element_type=f32
            )
            top = jnp.max(scores, axis=0, keepdims=True)
            weights = jnp.exp2((scores - top) * scale)
            mass = jnp.sum(weights, axis=0, keepdims=True)
            mixed = jnp.dot(values_t[h], weights.astype(bf16), preferred_element_type=f32)
            mixed = mixed * (1.0 / mass)
            level = top * scale + jnp.log2(mass)
            p0 = level.astype(bf16).astype(f32)
            rest = level - p0
            p1 = rest.astype(bf16).astype(f32)
            p2 = rest - p1
            for g in range(tile // 128):
                lanes = slice(g * 128, (g + 1) * 128)
                turned = mixed[:, lanes].T
                row = lax.broadcasted_iota(i32, (128, HEAD_DIM), 0) % SLOT_PAD
                turned = jnp.where(row == 28, p0[:, lanes], turned)
                turned = jnp.where(row == 29, p1[:, lanes], turned)
                turned = jnp.where(row == 30, p2[:, lanes], turned)
                out_ref[pl.ds(t * blocks + g * 4, 4), :, cols] = turned.astype(bf16).reshape(
                    4, SLOT_PAD, HEAD_DIM
                )
        return 0

    lax.fori_loop(0, q_ref.shape[0] // blocks, step, 0)


def fold(rows):
    half = rows.shape[1] // 2
    return jnp.concatenate([rows[:, :half], rows[:, half:]], axis=0)


def unfold(folded):
    count = folded.shape[0] // 2
    return jnp.concatenate([folded[:count], folded[count:]], axis=1)


def combine_kernel(parts_ref, rows_ref, mod_ref, hidden_ref, normed_ref, mark_ref, levels, turned):
    slots = rows_ref.shape[1]
    place = 2 * lax.rem(lax.axis_index("x"), 2) + lax.axis_index("core")
    heads = 24

    def source(part, group):
        return part * 8 + group * 2 if group < 4 else (group - 4) * 8 + part * 2 + 1

    for part in range(4):
        for group in range(8):
            tail = parts_ref[source(part, group), 24:32, :].astype(f32)
            level = tail[4:5] + tail[5:6] + tail[6:7]
            for h in range(HEADS_HERE):
                at = part * heads + group * HEADS_HERE + h
                levels[at : at + 1, :] = level[:, h * HEAD_DIM : (h + 1) * HEAD_DIM]
    pieces = [levels[p * heads : (p + 1) * heads, :] for p in range(4)]
    top = jnp.maximum(jnp.maximum(pieces[0], pieces[1]), jnp.maximum(pieces[2], pieces[3]))
    weights = [jnp.exp2(piece - top) for piece in pieces]
    total = 1.0 / (weights[0] + weights[1] + weights[2] + weights[3])
    for p in range(4):
        levels[p * heads : (p + 1) * heads, :] = weights[p] * total
    levels[4 * heads :, :] = jnp.zeros((128 - 4 * heads, 128), f32)
    turned[...] = levels[...].T
    mine = turned[pl.ds(pl.multiple_of(place * SLOT_PAD, SLOT_PAD), SLOT_PAD), :]
    shifts = mod_ref[0].astype(f32)
    for group in range(8):
        for h in range(HEADS_HERE):
            head = group * HEADS_HERE + h
            acc = jnp.zeros((SLOT_PAD, HEAD_DIM), f32)
            for part in range(4):
                column = part * heads + head
                block = parts_ref[source(part, group), :, h * HEAD_DIM : (h + 1) * HEAD_DIM]
                acc = acc + mine[:, column : column + 1] * block.astype(f32)
            cols = slice(head * HEAD_DIM, (head + 1) * HEAD_DIM)
            attended = acc[:slots] * shifts[2:3, cols]
            hidden_ref[:, cols] = rows_ref[0, :, cols].astype(f32) + attended
    hidden = hidden_ref[...]
    center = hidden - jnp.mean(hidden, axis=1, keepdims=True)
    spread = jnp.mean(center * center, axis=1, keepdims=True)
    normed = center * lax.rsqrt(spread + EPS) * (1.0 + shifts[1:2]) + shifts[0:1]
    normed_ref[...] = fold(normed).astype(bf16)
    mark_ref[...] = jnp.zeros(mark_ref.shape, bf16)


def load_kernel(after_ref, *refs):
    count = len(refs) // 2
    fetch(list(zip(refs[:count], refs[count : 2 * count])), refs[2 * count])


def load(after, arrays, limit):
    return call(
        load_kernel,
        [jax.ShapeDtypeStruct(v.shape, bf16) for v in arrays],
        scratch=[pltpu.SemaphoreType.DMA((len(arrays),))],
        n_in=1 + len(arrays),
        hbm=range(1 + len(arrays)),
        limit=limit,
        us=3.6,
    )(after, *arrays)


def feed_kernel(
    r0_ref, r1_ref, r2_ref, r3_ref, up_ref, b_up_ref, down_ref, o0, o1, o2, o3, rows_ref, active, terms
):
    chunk = 512
    slots = r0_ref.shape[0] // 2
    none = jnp.zeros((SLOT_PAD - slots, rows_ref.shape[1]), f32)
    for i, ref in enumerate((r0_ref, r1_ref, r2_ref, r3_ref)):
        block = jnp.concatenate([unfold(ref[...].astype(f32)), none], axis=0)
        rows_ref[i * SLOT_PAD : (i + 1) * SLOT_PAD, :] = block.astype(bf16)
    rows = rows_ref[...]
    for start in range(0, up_ref.shape[1], chunk):
        cols = slice(start, start + chunk)
        lifted = jnp.dot(rows, up_ref[:, cols], preferred_element_type=f32)
        lifted = lifted + b_up_ref[:, cols].astype(f32)
        active[:, cols] = jax.nn.gelu(lifted, approximate=True).astype(bf16)
    for start in range(0, down_ref.shape[1], chunk):
        cols = slice(start, start + chunk)
        terms[:, cols] = jnp.dot(active[...], down_ref[:, cols], preferred_element_type=f32)
    for i, out_ref in enumerate((o0, o1, o2, o3)):
        out_ref[...] = fold(terms[i * SLOT_PAD : i * SLOT_PAD + slots, :]).astype(bf16)


def finish_kernel(count_ref, t0_ref, t1_ref, t2_ref, t3_ref, hidden_ref, mod_ref, b_down_ref, out_ref):
    total = t0_ref[...].astype(f32)
    for ref in (t1_ref, t2_ref, t3_ref):
        total = total + ref[...].astype(f32)
    feed_out = unfold(total) + b_down_ref[...].astype(f32)
    result = hidden_ref[...] + mod_ref[0, 3:4].astype(f32) * feed_out
    live = lax.broadcasted_iota(i32, result.shape, 0) < count_ref[0, 0]
    out_ref[0] = jnp.where(live, result, 0.0).astype(bf16)


def position(z, x, core):
    return (z % 4) * 8 + (x % 4) * 2 + core


def ring_pairs(k):
    return [
        (position(z, x, c), position(z, x + k, 0) if c == 0 else position(z + k, x, 1))
        for z in range(4)
        for x in range(4)
        for c in range(2)
    ]


def turn(k):
    return [(y, (y + k) % 4) for y in range(4)]


def body(rows_in, fresh_qkv, kv_cache, chosen, counts, modulation, w_up, b_up, w_down, b_down):
    shape = jax.ShapeDtypeStruct
    slots, width = rows_in.shape[1], rows_in.shape[2]
    tokens = kv_cache.shape[1]
    fresh = jnp.swapaxes(fresh_qkv[0], 0, 1)
    q_blocks, keep, send = pl.pallas_call(
        pack_kernel,
        out_shape=[shape((32, SLOT_PAD, BLOCK), bf16)] + [shape((4, 2, tokens, BLOCK), bf16)] * 2,
        in_specs=[pl.BlockSpec(memory_space=pltpu.SMEM)] + [pl.BlockSpec(memory_space=pltpu.HBM)] * 3,
        out_specs=[pl.BlockSpec(memory_space=pltpu.HBM)] * 3,
        scratch_shapes=[
            pltpu.VMEM((tokens, 2, width), bf16),
            pltpu.VMEM((3, slots, width), bf16),
            pltpu.VMEM((1, slots), i32),
            pltpu.VMEM((2, tokens, width), bf16),
            pltpu.VMEM((32, SLOT_PAD, BLOCK), bf16),
            pltpu.SemaphoreType.DMA((4,)),
            pltpu.SemaphoreType.DMA((17,)),
        ],
        compiler_params=pltpu.CompilerParams(vmem_limit_bytes=61 * MB),
    )(counts, kv_cache[0], fresh, chosen)
    q_all = lax.all_to_all(q_blocks, SEQ, 0, 0, tiled=True)
    swap = [(position(z, x, c), position(z, x, 1 - c)) for z in range(4) for x in range(4) for c in range(2)]
    first = lax.ppermute(send, SEQ, swap)
    stacked = call(stack_kernel, [shape((2, 2, tokens, BLOCK), bf16)] * 4, n_in=2)(keep, first)
    others = [lax.ppermute(stacked[k], SEQ, ring_pairs(k)) for k in (1, 2, 3)]

    partial = call(
        attention_kernel,
        shape((32, SLOT_PAD, BLOCK), bf16),
        scratch=[pltpu.VMEM((8 * tokens, BLOCK), bf16), pltpu.VMEM((HEADS_HERE, HEAD_DIM, 8 * tokens), bf16)],
        n_in=5,
        limit=24,
        us=6.5,
    )(q_all, stacked[0], *others)
    parts = lax.all_to_all(partial, SEQ, 0, 0, tiled=True)
    rows, mod = load(partial, [rows_in, modulation], 16)
    hidden, normed, mark = call(
        combine_kernel,
        [shape((slots, width), f32), shape((2 * slots, width // 2), bf16), shape((16, 128), bf16)],
        scratch=[pltpu.VMEM((128, 128), f32), pltpu.VMEM((128, 128), f32)],
        n_in=3,
        us=1.6,
    )(parts, rows, mod)

    visits = [lax.ppermute(normed, "y", turn(k)) for k in (1, 2, 3)]
    up, down = load(mark, [w_up, w_down], 34)
    terms = call(
        feed_kernel,
        [shape((2 * slots, width // 2), bf16)] * 4,
        scratch=[
            pltpu.VMEM((4 * SLOT_PAD, width), bf16),
            pltpu.VMEM((4 * SLOT_PAD, w_up.shape[1]), bf16),
            pltpu.VMEM((4 * SLOT_PAD, width), f32),
        ],
        n_in=7,
        us=3.7,
    )(normed, *visits, up, b_up[None], down)
    back = [lax.ppermute(terms[k], "y", turn(-k)) for k in (1, 2, 3)]
    return call(finish_kernel, shape((1, slots, width), bf16), n_in=8, smem=(0,), us=1.4)(
        counts, terms[0], *back, hidden, modulation, b_down[None]
    )


def solution(mesh):
    whole = jax.sharding.Mesh(mesh.devices.reshape(4, 4, 4, 2), ("y", "z", "x", "core"))
    placed = (
        P("y", SEQ, None),
        P("y", SEQ, None, None),
        P("y", SEQ, None, None),
        P("y", SEQ),
        P("y", SEQ),
        P("y", None, None),
        P(None, "y"),
        P("y"),
        P("y", None),
        P(),
    )
    return jax.shard_map(body, mesh=whole, in_specs=placed, out_specs=P("y", SEQ, None), check_vma=False)
```

```python
import jax
import jax.numpy as jnp
from jax import lax
from jax.experimental import pallas as pl
from jax.experimental.pallas import tpu as pltpu
from jax.sharding import PartitionSpec as P

HEAD_DIM = 128
HEADS_HERE = 3
BLOCK = HEADS_HERE * HEAD_DIM
SLOT_PAD = 32
LOG2E = 1.4426950408889634
EPS = 1e-06
SEQ = ("z", "x", "core")
bf16 = jnp.bfloat16
f32 = jnp.float32
i32 = jnp.int32
MB = 1 << 20


def call(kernel, out_shape, scratch=(), limit=16, smem=(), hbm=(), n_in=None, us=1.0):
    def space(i):
        return pltpu.SMEM if i in smem else pltpu.HBM if i in hbm else pltpu.VMEM

    return pl.pallas_call(
        kernel,
        out_shape=out_shape,
        in_specs=[pl.BlockSpec(memory_space=space(i)) for i in range(n_in)],
        scratch_shapes=list(scratch),
        compiler_params=pltpu.CompilerParams(vmem_limit_bytes=limit * MB),
        cost_estimate=pl.CostEstimate(flops=0, transcendentals=0, bytes_accessed=int(us * 3.3e6)),
    )


def fetch(pairs, sems):
    copies = [pltpu.make_async_copy(src, dst, sems.at[i]) for i, (src, dst) in enumerate(pairs)]
    for copy in copies:
        copy.start()
    for copy in copies:
        copy.wait()


def pack_kernel(
    count_ref, kv_hbm, fresh_hbm, chosen_hbm, keep_hbm, send_hbm,
    kv_ref, fresh_ref, chosen_ref, patched, queries, in_sems, out_sems,
):
    sources = [
        (fresh_hbm.at[0], fresh_ref.at[0]),
        (kv_hbm, kv_ref),
        (fresh_hbm.at[1:3], fresh_ref.at[1:3]),
        (chosen_hbm, chosen_ref),
    ]
    copies = [pltpu.make_async_copy(src, dst, in_sems.at[i]) for i, (src, dst) in enumerate(sources)]
    for copy in copies:
        copy.start()
    tokens = kv_ref.shape[0]
    slots = fresh_ref.shape[1]
    core, ring_x, ring_z = (lax.axis_index(a) for a in ("core", "x", "z"))
    count = count_ref[0, 0]
    half = 4 * BLOCK
    outs = []

    def send_out(source, first_row, rows, k, mine, other):
        at_mine = pl.multiple_of(core * half + mine * BLOCK, BLOCK)
        at_other = pl.multiple_of((1 - core) * half + other * BLOCK, BLOCK)
        for at, target in ((at_other, send_hbm), (at_mine, keep_hbm)):
            copy = pltpu.make_async_copy(
                source.at[:, pl.ds(at, BLOCK)],
                target.at[k, pl.ds(first_row, rows)],
                out_sems.at[len(outs)],
            )
            copy.start()
            outs.append(copy)

    copies[0].wait()
    queries[:slots, :] = fresh_ref[0]
    queries[slots:, :] = jnp.zeros((SLOT_PAD - slots, queries.shape[1]), bf16)
    for k in range(4):
        send_out(queries, 2 * tokens, SLOT_PAD, k, k, k)
    for copy in copies[1:]:
        copy.wait()
    token_id = lax.broadcasted_iota(i32, (tokens, slots), 0)
    slot_id = lax.broadcasted_iota(i32, (tokens, slots), 1)
    hit = (token_id == chosen_ref[...]) & (slot_id < count)
    hot = jnp.where(hit, 1.0, 0.0)
    taken = jnp.sum(hot, axis=1, keepdims=True) > 0.5
    hot = hot.astype(bf16)
    old = jnp.swapaxes(kv_ref[...], 0, 1)
    for which in range(2):
        new = jnp.dot(hot, fresh_ref[1 + which], preferred_element_type=f32)
        patched[which] = jnp.where(taken, new, old[which].astype(f32)).astype(bf16)
        for k in range(4):
            mine = lax.rem(jnp.where(core == 0, ring_x, ring_z) + k, 4)
            other = lax.rem(jnp.where(core == 0, ring_z, ring_x) + k, 4)
            send_out(patched.at[which], which * tokens, tokens, k, mine, other)
    for copy in outs:
        copy.wait()


def stack_kernel(keep_ref, first_ref, *refs):
    core = lax.axis_index("core")
    rows = refs[0].shape[1]
    for k, out_ref in enumerate(refs[:4]):
        out_ref[0] = keep_ref[k, :rows]
        out_ref[1] = first_ref[k, :rows]
    q_ref = refs[4]
    for chip in range(16):
        group = jnp.where(core == 0, chip % 4, chip // 4)
        q_ref[chip, core] = keep_ref[group, rows:]
        q_ref[chip, 1 - core] = first_ref[group, rows:]


def gather_keys(sources, keys, values_t):
    rows = 128
    at = 0
    for ref in sources:
        for core in range(2):
            keys[at : at + rows, :] = ref[core, :rows, :]
            for h in range(HEADS_HERE):
                cols = slice(h * HEAD_DIM, (h + 1) * HEAD_DIM)
                values_t[h, :, at : at + rows] = ref[core, rows:, cols].T
            at += rows


def head_scores(q_all, keys, h):
    cols = slice(h * HEAD_DIM, (h + 1) * HEAD_DIM)
    return lax.dot_general(
        keys[:, cols], q_all[:, cols], (((1,), (1,)), ((), ())), preferred_element_type=f32
    )


SCALE = LOG2E * HEAD_DIM**-0.5


def attention_first_kernel(q_ref, r0_ref, r1_ref, mixed_ref, stats_ref, keys, values_t):
    gather_keys((r0_ref, r1_ref), keys, values_t)
    q_all = q_ref[...].reshape(-1, BLOCK)
    for h in range(HEADS_HERE):
        scores = head_scores(q_all, keys, h)
        top = jnp.max(scores, axis=0, keepdims=True)
        weights = jnp.exp2((scores - top) * SCALE)
        stats_ref[h : h + 1, :] = top
        stats_ref[4 + h : 5 + h, :] = jnp.sum(weights, axis=0, keepdims=True)
        mixed_ref[h] = jnp.dot(values_t[h], weights.astype(bf16), preferred_element_type=f32)


def attention_second_kernel(q_ref, r2_ref, r3_ref, mixed_ref, stats_ref, out_ref, keys, values_t):
    gather_keys((r2_ref, r3_ref), keys, values_t)
    q_all = q_ref[...].reshape(-1, BLOCK)
    for h in range(HEADS_HERE):
        cols = slice(h * HEAD_DIM, (h + 1) * HEAD_DIM)
        scores = head_scores(q_all, keys, h)
        before = stats_ref[h : h + 1, :]
        top = jnp.maximum(jnp.max(scores, axis=0, keepdims=True), before)
        weights = jnp.exp2((scores - top) * SCALE)
        shrink = jnp.exp2((before - top) * SCALE)
        mass = jnp.sum(weights, axis=0, keepdims=True) + shrink * stats_ref[4 + h : 5 + h, :]
        mixed = jnp.dot(values_t[h], weights.astype(bf16), preferred_element_type=f32)
        mixed = (mixed + shrink * mixed_ref[h]) * (1.0 / mass)
        level = top * SCALE + jnp.log2(mass)
        p0 = level.astype(bf16).astype(f32)
        rest = level - p0
        p1 = rest.astype(bf16).astype(f32)
        p2 = rest - p1
        for g in range(q_all.shape[0] // 128):
            lanes = slice(g * 128, (g + 1) * 128)
            turned = mixed[:, lanes].T
            row = lax.broadcasted_iota(i32, (128, HEAD_DIM), 0) % SLOT_PAD
            turned = jnp.where(row == 28, p0[:, lanes], turned)
            turned = jnp.where(row == 29, p1[:, lanes], turned)
            turned = jnp.where(row == 30, p2[:, lanes], turned)
            out_ref[g * 4 : (g + 1) * 4, :, cols] = turned.astype(bf16).reshape(4, SLOT_PAD, HEAD_DIM)


def fold(rows):
    half = rows.shape[1] // 2
    return jnp.concatenate([rows[:, :half], rows[:, half:]], axis=0)


def unfold(folded):
    count = folded.shape[0] // 2
    return jnp.concatenate([folded[:count], folded[count:]], axis=1)


def combine_kernel(parts_ref, rows_ref, mod_ref, hidden_ref, normed_ref, mark_ref, levels, turned):
    slots = rows_ref.shape[1]
    place = 2 * lax.rem(lax.axis_index("x"), 2) + lax.axis_index("core")
    heads = 24

    def source(part, group):
        return part * 8 + group * 2 if group < 4 else (group - 4) * 8 + part * 2 + 1

    for part in range(4):
        for group in range(8):
            tail = parts_ref[source(part, group), 24:32, :].astype(f32)
            level = tail[4:5] + tail[5:6] + tail[6:7]
            for h in range(HEADS_HERE):
                at = part * heads + group * HEADS_HERE + h
                levels[at : at + 1, :] = level[:, h * HEAD_DIM : (h + 1) * HEAD_DIM]
    pieces = [levels[p * heads : (p + 1) * heads, :] for p in range(4)]
    top = jnp.maximum(jnp.maximum(pieces[0], pieces[1]), jnp.maximum(pieces[2], pieces[3]))
    weights = [jnp.exp2(piece - top) for piece in pieces]
    total = 1.0 / (weights[0] + weights[1] + weights[2] + weights[3])
    for p in range(4):
        levels[p * heads : (p + 1) * heads, :] = weights[p] * total
    levels[4 * heads :, :] = jnp.zeros((128 - 4 * heads, 128), f32)
    turned[...] = levels[...].T
    mine = turned[pl.ds(pl.multiple_of(place * SLOT_PAD, SLOT_PAD), SLOT_PAD), :]
    shifts = mod_ref[0].astype(f32)
    for group in range(8):
        for h in range(HEADS_HERE):
            head = group * HEADS_HERE + h
            acc = jnp.zeros((SLOT_PAD, HEAD_DIM), f32)
            for part in range(4):
                column = part * heads + head
                block = parts_ref[source(part, group), :, h * HEAD_DIM : (h + 1) * HEAD_DIM]
                acc = acc + mine[:, column : column + 1] * block.astype(f32)
            cols = slice(head * HEAD_DIM, (head + 1) * HEAD_DIM)
            attended = acc[:slots] * shifts[2:3, cols]
            hidden_ref[:, cols] = rows_ref[0, :, cols].astype(f32) + attended
    hidden = hidden_ref[...]
    center = hidden - jnp.mean(hidden, axis=1, keepdims=True)
    spread = jnp.mean(center * center, axis=1, keepdims=True)
    normed = center * lax.rsqrt(spread + EPS) * (1.0 + shifts[1:2]) + shifts[0:1]
    normed_ref[...] = fold(normed).astype(bf16)
    mark_ref[...] = jnp.zeros(mark_ref.shape, bf16)


def load_kernel(after_ref, *refs):
    count = len(refs) // 2
    fetch(list(zip(refs[:count], refs[count : 2 * count])), refs[2 * count])


def load(after, arrays, limit):
    return call(
        load_kernel,
        [jax.ShapeDtypeStruct(v.shape, bf16) for v in arrays],
        scratch=[pltpu.SemaphoreType.DMA((len(arrays),))],
        n_in=1 + len(arrays),
        hbm=range(1 + len(arrays)),
        limit=limit,
        us=3.6,
    )(after, *arrays)


def feed_kernel(
    r0_ref, r1_ref, r2_ref, r3_ref, up_ref, b_up_ref, down_ref, o0, o1, o2, o3, rows_ref, active, terms
):
    chunk = 512
    slots = r0_ref.shape[0] // 2
    none = jnp.zeros((SLOT_PAD - slots, rows_ref.shape[1]), f32)
    for i, ref in enumerate((r0_ref, r1_ref, r2_ref, r3_ref)):
        block = jnp.concatenate([unfold(ref[...].astype(f32)), none], axis=0)
        rows_ref[i * SLOT_PAD : (i + 1) * SLOT_PAD, :] = block.astype(bf16)
    rows = rows_ref[...]
    for start in range(0, up_ref.shape[1], chunk):
        cols = slice(start, start + chunk)
        lifted = jnp.dot(rows, up_ref[:, cols], preferred_element_type=f32)
        lifted = lifted + b_up_ref[:, cols].astype(f32)
        active[:, cols] = jax.nn.gelu(lifted, approximate=True).astype(bf16)
    for start in range(0, down_ref.shape[1], chunk):
        cols = slice(start, start + chunk)
        terms[:, cols] = jnp.dot(active[...], down_ref[:, cols], preferred_element_type=f32)
    for i, out_ref in enumerate((o0, o1, o2, o3)):
        out_ref[...] = fold(terms[i * SLOT_PAD : i * SLOT_PAD + slots, :]).astype(bf16)


def finish_kernel(count_ref, t0_ref, t1_ref, t2_ref, t3_ref, hidden_ref, mod_ref, b_down_ref, out_ref):
    total = t0_ref[...].astype(f32)
    for ref in (t1_ref, t2_ref, t3_ref):
        total = total + ref[...].astype(f32)
    feed_out = unfold(total) + b_down_ref[...].astype(f32)
    result = hidden_ref[...] + mod_ref[0, 3:4].astype(f32) * feed_out
    live = lax.broadcasted_iota(i32, result.shape, 0) < count_ref[0, 0]
    out_ref[0] = jnp.where(live, result, 0.0).astype(bf16)


def position(z, x, core):
    return (z % 4) * 8 + (x % 4) * 2 + core


def ring_pairs(k):
    return [
        (position(z, x, c), position(z, x + k, 0) if c == 0 else position(z + k, x, 1))
        for z in range(4)
        for x in range(4)
        for c in range(2)
    ]


def turn(k):
    return [(y, (y + k) % 4) for y in range(4)]


def body(rows_in, fresh_qkv, kv_cache, chosen, counts, modulation, w_up, b_up, w_down, b_down):
    shape = jax.ShapeDtypeStruct
    slots, width = rows_in.shape[1], rows_in.shape[2]
    tokens = kv_cache.shape[1]
    fresh = jnp.swapaxes(fresh_qkv[0], 0, 1)
    packed = shape((4, 2 * tokens + SLOT_PAD, BLOCK), bf16)
    keep, send = pl.pallas_call(
        pack_kernel,
        out_shape=[packed] * 2,
        in_specs=[pl.BlockSpec(memory_space=pltpu.SMEM)] + [pl.BlockSpec(memory_space=pltpu.HBM)] * 3,
        out_specs=[pl.BlockSpec(memory_space=pltpu.HBM)] * 2,
        scratch_shapes=[
            pltpu.VMEM((tokens, 2, width), bf16),
            pltpu.VMEM((3, slots, width), bf16),
            pltpu.VMEM((1, slots), i32),
            pltpu.VMEM((2, tokens, width), bf16),
            pltpu.VMEM((SLOT_PAD, width), bf16),
            pltpu.SemaphoreType.DMA((4,)),
            pltpu.SemaphoreType.DMA((24,)),
        ],
        compiler_params=pltpu.CompilerParams(vmem_limit_bytes=61 * MB),
    )(counts, kv_cache[0], fresh, chosen)
    swap = [(position(z, x, c), position(z, x, 1 - c)) for z in range(4) for x in range(4) for c in range(2)]
    first = lax.ppermute(send, SEQ, swap)
    *stacked, q_blocks = call(
        stack_kernel,
        [shape((2, 2 * tokens, BLOCK), bf16)] * 4 + [shape((16, 2, SLOT_PAD, BLOCK), bf16)],
        n_in=2,
    )(keep, first)
    others = [lax.ppermute(stacked[k], SEQ, ring_pairs(k)) for k in (1, 2, 3)]
    q_all = lax.all_to_all(q_blocks.reshape(16, 2 * SLOT_PAD, BLOCK), ("z", "x"), 0, 0, tiled=True)
    q_all = q_all.reshape(32, SLOT_PAD, BLOCK)

    rows = 32 * SLOT_PAD
    scratch = [pltpu.VMEM((4 * tokens, BLOCK), bf16), pltpu.VMEM((HEADS_HERE, HEAD_DIM, 4 * tokens), bf16)]
    mixed, stats = call(
        attention_first_kernel,
        [shape((HEADS_HERE, HEAD_DIM, rows), f32), shape((8, rows), f32)],
        scratch=scratch,
        n_in=3,
        limit=24,
        us=2.8,
    )(q_all, stacked[0], others[0])
    partial = call(
        attention_second_kernel,
        shape((32, SLOT_PAD, BLOCK), bf16),
        scratch=scratch,
        n_in=5,
        limit=24,
        us=3.0,
    )(q_all, others[1], others[2], mixed, stats)
    parts = lax.all_to_all(partial, SEQ, 0, 0, tiled=True)
    rows, mod = load(partial, [rows_in, modulation], 16)
    hidden, normed, mark = call(
        combine_kernel,
        [shape((slots, width), f32), shape((2 * slots, width // 2), bf16), shape((16, 128), bf16)],
        scratch=[pltpu.VMEM((128, 128), f32), pltpu.VMEM((128, 128), f32)],
        n_in=3,
        us=1.6,
    )(parts, rows, mod)

    far, near, last = (lax.ppermute(normed, "y", turn(k)) for k in (2, 1, 3))
    visits = [near, far, last]
    up, down = load(mark, [w_up, w_down], 34)
    terms = call(
        feed_kernel,
        [shape((2 * slots, width // 2), bf16)] * 4,
        scratch=[
            pltpu.VMEM((4 * SLOT_PAD, width), bf16),
            pltpu.VMEM((4 * SLOT_PAD, w_up.shape[1]), bf16),
            pltpu.VMEM((4 * SLOT_PAD, width), f32),
        ],
        n_in=7,
        us=3.7,
    )(normed, *visits, up, b_up[None], down)
    back = [lax.ppermute(terms[k], "y", turn(-k)) for k in (2, 1, 3)]
    return call(finish_kernel, shape((1, slots, width), bf16), n_in=8, smem=(0,), us=1.4)(
        counts, terms[0], *back, hidden, modulation, b_down[None]
    )


def solution(mesh):
    whole = jax.sharding.Mesh(mesh.devices.reshape(4, 4, 4, 2), ("y", "z", "x", "core"))
    placed = (
        P("y", SEQ, None),
        P("y", SEQ, None, None),
        P("y", SEQ, None, None),
        P("y", SEQ),
        P("y", SEQ),
        P("y", None, None),
        P(None, "y"),
        P("y"),
        P("y", None),
        P(),
    )
    return jax.shard_map(body, mesh=whole, in_specs=placed, out_specs=P("y", SEQ, None), check_vma=False)
```

```python
import jax
import jax.numpy as jnp
from jax import lax
from jax.experimental import pallas as pl
from jax.experimental.pallas import tpu as pltpu
from jax.sharding import PartitionSpec as P

HEAD_DIM = 128
HEADS_HERE = 3
BLOCK = HEADS_HERE * HEAD_DIM
SLOT_PAD = 32
LOG2E = 1.4426950408889634
EPS = 1e-06
SEQ = ("z", "x", "core")
bf16 = jnp.bfloat16
f32 = jnp.float32
i32 = jnp.int32
MB = 1 << 20


def call(kernel, out_shape, scratch=(), limit=16, smem=(), hbm=(), n_in=None, us=1.0):
    def space(i):
        return pltpu.SMEM if i in smem else pltpu.HBM if i in hbm else pltpu.VMEM

    return pl.pallas_call(
        kernel,
        out_shape=out_shape,
        in_specs=[pl.BlockSpec(memory_space=space(i)) for i in range(n_in)],
        scratch_shapes=list(scratch),
        compiler_params=pltpu.CompilerParams(vmem_limit_bytes=limit * MB),
        cost_estimate=pl.CostEstimate(flops=0, transcendentals=0, bytes_accessed=int(us * 3.3e6)),
    )


def fetch(pairs, sems):
    copies = [pltpu.make_async_copy(src, dst, sems.at[i]) for i, (src, dst) in enumerate(pairs)]
    for copy in copies:
        copy.start()
    for copy in copies:
        copy.wait()


def pack_kernel(
    count_ref, kv_hbm, fresh_hbm, chosen_hbm, q_hbm, keep_hbm, send_hbm,
    kv_ref, fresh_ref, chosen_ref, patched, q_out, in_sems, out_sems,
):
    sources = [
        (fresh_hbm.at[0], fresh_ref.at[0]),
        (kv_hbm, kv_ref),
        (fresh_hbm.at[1:3], fresh_ref.at[1:3]),
        (chosen_hbm, chosen_ref),
    ]
    copies = [pltpu.make_async_copy(src, dst, in_sems.at[i]) for i, (src, dst) in enumerate(sources)]
    for copy in copies:
        copy.start()
    tokens = kv_ref.shape[0]
    slots = fresh_ref.shape[1]
    copies[0].wait()
    for dest in range(32):
        z, x, core = dest // 8, dest // 2 % 4, dest % 2
        group = x if core == 0 else 4 + z
        q_out[dest, :slots, :] = fresh_ref[0, :, group * BLOCK : (group + 1) * BLOCK]
        q_out[dest, slots:, :] = jnp.zeros((SLOT_PAD - slots, BLOCK), bf16)
    outs = [pltpu.make_async_copy(q_out, q_hbm, out_sems.at[0])]
    outs[0].start()

    core, ring_x, ring_z = (lax.axis_index(a) for a in ("core", "x", "z"))
    count = count_ref[0, 0]
    for copy in copies[1:]:
        copy.wait()
    token_id = lax.broadcasted_iota(i32, (tokens, slots), 0)
    slot_id = lax.broadcasted_iota(i32, (tokens, slots), 1)
    hit = (token_id == chosen_ref[...]) & (slot_id < count)
    hot = jnp.where(hit, 1.0, 0.0)
    taken = jnp.sum(hot, axis=1, keepdims=True) > 0.5
    hot = hot.astype(bf16)
    old = jnp.swapaxes(kv_ref[...], 0, 1)
    half = 4 * BLOCK
    for which in range(2):
        new = jnp.dot(hot, fresh_ref[1 + which], preferred_element_type=f32)
        patched[which] = jnp.where(taken, new, old[which].astype(f32)).astype(bf16)
        for k in range(4):
            mine = lax.rem(jnp.where(core == 0, ring_x, ring_z) + k, 4)
            other = lax.rem(jnp.where(core == 0, ring_z, ring_x) + k, 4)
            at_mine = pl.multiple_of(core * half + mine * BLOCK, BLOCK)
            at_other = pl.multiple_of((1 - core) * half + other * BLOCK, BLOCK)
            for at, target in ((at_other, send_hbm), (at_mine, keep_hbm)):
                copy = pltpu.make_async_copy(
                    patched.at[which, :, pl.ds(at, BLOCK)], target.at[k, which], out_sems.at[len(outs)]
                )
                copy.start()
                outs.append(copy)
    for copy in outs:
        copy.wait()


def stack_kernel(keep_ref, first_ref, *out_refs):
    for k, out_ref in enumerate(out_refs):
        out_ref[0] = keep_ref[k]
        out_ref[1] = first_ref[k]


def gather_keys(sources, keys, values_t):
    rows = 128
    at = 0
    for ref in sources:
        for core in range(2):
            keys[at : at + rows, :] = ref[core, 0]
            for h in range(HEADS_HERE):
                cols = slice(h * HEAD_DIM, (h + 1) * HEAD_DIM)
                values_t[h, :, at : at + rows] = ref[core, 1, :, cols].T
            at += rows


def head_scores(q_all, keys, h):
    cols = slice(h * HEAD_DIM, (h + 1) * HEAD_DIM)
    return lax.dot_general(
        keys[:, cols], q_all[:, cols], (((1,), (1,)), ((), ())), preferred_element_type=f32
    )


SCALE = LOG2E * HEAD_DIM**-0.5


def attention_first_kernel(q_ref, r0_ref, r1_ref, mixed_ref, stats_ref, keys, values_t):
    gather_keys((r0_ref, r1_ref), keys, values_t)
    q_all = q_ref[...].reshape(-1, BLOCK)
    for h in range(HEADS_HERE):
        scores = head_scores(q_all, keys, h)
        top = jnp.max(scores, axis=0, keepdims=True)
        weights = jnp.exp2((scores - top) * SCALE)
        stats_ref[h : h + 1, :] = top
        stats_ref[4 + h : 5 + h, :] = jnp.sum(weights, axis=0, keepdims=True)
        mixed_ref[h] = jnp.dot(values_t[h], weights.astype(bf16), preferred_element_type=f32)


def attention_second_kernel(q_ref, r2_ref, r3_ref, mixed_ref, stats_ref, out_ref, keys, values_t):
    gather_keys((r2_ref, r3_ref), keys, values_t)
    q_all = q_ref[...].reshape(-1, BLOCK)
    for h in range(HEADS_HERE):
        cols = slice(h * HEAD_DIM, (h + 1) * HEAD_DIM)
        scores = head_scores(q_all, keys, h)
        before = stats_ref[h : h + 1, :]
        top = jnp.maximum(jnp.max(scores, axis=0, keepdims=True), before)
        weights = jnp.exp2((scores - top) * SCALE)
        shrink = jnp.exp2((before - top) * SCALE)
        mass = jnp.sum(weights, axis=0, keepdims=True) + shrink * stats_ref[4 + h : 5 + h, :]
        mixed = jnp.dot(values_t[h], weights.astype(bf16), preferred_element_type=f32)
        mixed = (mixed + shrink * mixed_ref[h]) * (1.0 / mass)
        level = top * SCALE + jnp.log2(mass)
        p0 = level.astype(bf16).astype(f32)
        rest = level - p0
        p1 = rest.astype(bf16).astype(f32)
        p2 = rest - p1
        for g in range(q_all.shape[0] // 128):
            lanes = slice(g * 128, (g + 1) * 128)
            turned = mixed[:, lanes].T
            row = lax.broadcasted_iota(i32, (128, HEAD_DIM), 0) % SLOT_PAD
            turned = jnp.where(row == 28, p0[:, lanes], turned)
            turned = jnp.where(row == 29, p1[:, lanes], turned)
            turned = jnp.where(row == 30, p2[:, lanes], turned)
            out_ref[g * 4 : (g + 1) * 4, :, cols] = turned.astype(bf16).reshape(4, SLOT_PAD, HEAD_DIM)


def fold(rows):
    half = rows.shape[1] // 2
    return jnp.concatenate([rows[:, :half], rows[:, half:]], axis=0)


def unfold(folded):
    count = folded.shape[0] // 2
    return jnp.concatenate([folded[:count], folded[count:]], axis=1)


def combine_kernel(parts_ref, rows_ref, mod_ref, hidden_ref, normed_ref, mark_ref, levels, turned):
    slots = rows_ref.shape[1]
    place = 2 * lax.rem(lax.axis_index("x"), 2) + lax.axis_index("core")
    heads = 24

    def source(part, group):
        return part * 8 + group * 2 if group < 4 else (group - 4) * 8 + part * 2 + 1

    for part in range(4):
        for group in range(8):
            tail = parts_ref[source(part, group), 24:32, :].astype(f32)
            level = tail[4:5] + tail[5:6] + tail[6:7]
            for h in range(HEADS_HERE):
                at = part * heads + group * HEADS_HERE + h
                levels[at : at + 1, :] = level[:, h * HEAD_DIM : (h + 1) * HEAD_DIM]
    pieces = [levels[p * heads : (p + 1) * heads, :] for p in range(4)]
    top = jnp.maximum(jnp.maximum(pieces[0], pieces[1]), jnp.maximum(pieces[2], pieces[3]))
    weights = [jnp.exp2(piece - top) for piece in pieces]
    total = 1.0 / (weights[0] + weights[1] + weights[2] + weights[3])
    for p in range(4):
        levels[p * heads : (p + 1) * heads, :] = weights[p] * total
    levels[4 * heads :, :] = jnp.zeros((128 - 4 * heads, 128), f32)
    turned[...] = levels[...].T
    mine = turned[pl.ds(pl.multiple_of(place * SLOT_PAD, SLOT_PAD), SLOT_PAD), :]
    shifts = mod_ref[0].astype(f32)
    for group in range(8):
        for h in range(HEADS_HERE):
            head = group * HEADS_HERE + h
            acc = jnp.zeros((SLOT_PAD, HEAD_DIM), f32)
            for part in range(4):
                column = part * heads + head
                block = parts_ref[source(part, group), :, h * HEAD_DIM : (h + 1) * HEAD_DIM]
                acc = acc + mine[:, column : column + 1] * block.astype(f32)
            cols = slice(head * HEAD_DIM, (head + 1) * HEAD_DIM)
            attended = acc[:slots] * shifts[2:3, cols]
            hidden_ref[:, cols] = rows_ref[0, :, cols].astype(f32) + attended
    hidden = hidden_ref[...]
    center = hidden - jnp.mean(hidden, axis=1, keepdims=True)
    spread = jnp.mean(center * center, axis=1, keepdims=True)
    normed = center * lax.rsqrt(spread + EPS) * (1.0 + shifts[1:2]) + shifts[0:1]
    normed_ref[...] = fold(normed).astype(bf16)
    mark_ref[...] = jnp.zeros(mark_ref.shape, bf16)


def load_kernel(after_ref, *refs):
    count = len(refs) // 2
    fetch(list(zip(refs[:count], refs[count : 2 * count])), refs[2 * count])


def load(after, arrays, limit):
    return call(
        load_kernel,
        [jax.ShapeDtypeStruct(v.shape, bf16) for v in arrays],
        scratch=[pltpu.SemaphoreType.DMA((len(arrays),))],
        n_in=1 + len(arrays),
        hbm=range(1 + len(arrays)),
        limit=limit,
        us=3.6,
    )(after, *arrays)


def feed_kernel(
    r0_ref, r1_ref, r2_ref, r3_ref, up_ref, b_up_ref, down_ref, o0, o1, o2, o3, rows_ref, active, terms
):
    chunk = 512
    slots = r0_ref.shape[0] // 2
    none = jnp.zeros((SLOT_PAD - slots, rows_ref.shape[1]), f32)
    for i, ref in enumerate((r0_ref, r1_ref, r2_ref, r3_ref)):
        block = jnp.concatenate([unfold(ref[...].astype(f32)), none], axis=0)
        rows_ref[i * SLOT_PAD : (i + 1) * SLOT_PAD, :] = block.astype(bf16)
    rows = rows_ref[...]
    for start in range(0, up_ref.shape[1], chunk):
        cols = slice(start, start + chunk)
        lifted = jnp.dot(rows, up_ref[:, cols], preferred_element_type=f32)
        lifted = lifted + b_up_ref[:, cols].astype(f32)
        active[:, cols] = jax.nn.gelu(lifted, approximate=True).astype(bf16)
    for start in range(0, down_ref.shape[1], chunk):
        cols = slice(start, start + chunk)
        terms[:, cols] = jnp.dot(active[...], down_ref[:, cols], preferred_element_type=f32)
    for i, out_ref in enumerate((o0, o1, o2, o3)):
        out_ref[...] = fold(terms[i * SLOT_PAD : i * SLOT_PAD + slots, :]).astype(bf16)


def finish_kernel(count_ref, t0_ref, t1_ref, t2_ref, t3_ref, hidden_ref, mod_ref, b_down_ref, out_ref):
    total = t0_ref[...].astype(f32)
    for ref in (t1_ref, t2_ref, t3_ref):
        total = total + ref[...].astype(f32)
    feed_out = unfold(total) + b_down_ref[...].astype(f32)
    result = hidden_ref[...] + mod_ref[0, 3:4].astype(f32) * feed_out
    live = lax.broadcasted_iota(i32, result.shape, 0) < count_ref[0, 0]
    out_ref[0] = jnp.where(live, result, 0.0).astype(bf16)


def position(z, x, core):
    return (z % 4) * 8 + (x % 4) * 2 + core


def ring_pairs(k):
    return [
        (position(z, x, c), position(z, x + k, 0) if c == 0 else position(z + k, x, 1))
        for z in range(4)
        for x in range(4)
        for c in range(2)
    ]


def turn(k):
    return [(y, (y + k) % 4) for y in range(4)]


def body(rows_in, fresh_qkv, kv_cache, chosen, counts, modulation, w_up, b_up, w_down, b_down):
    shape = jax.ShapeDtypeStruct
    slots, width = rows_in.shape[1], rows_in.shape[2]
    tokens = kv_cache.shape[1]
    fresh = jnp.swapaxes(fresh_qkv[0], 0, 1)
    q_blocks, keep, send = pl.pallas_call(
        pack_kernel,
        out_shape=[shape((32, SLOT_PAD, BLOCK), bf16)] + [shape((4, 2, tokens, BLOCK), bf16)] * 2,
        in_specs=[pl.BlockSpec(memory_space=pltpu.SMEM)] + [pl.BlockSpec(memory_space=pltpu.HBM)] * 3,
        out_specs=[pl.BlockSpec(memory_space=pltpu.HBM)] * 3,
        scratch_shapes=[
            pltpu.VMEM((tokens, 2, width), bf16),
            pltpu.VMEM((3, slots, width), bf16),
            pltpu.VMEM((1, slots), i32),
            pltpu.VMEM((2, tokens, width), bf16),
            pltpu.VMEM((32, SLOT_PAD, BLOCK), bf16),
            pltpu.SemaphoreType.DMA((4,)),
            pltpu.SemaphoreType.DMA((17,)),
        ],
        compiler_params=pltpu.CompilerParams(vmem_limit_bytes=61 * MB),
    )(counts, kv_cache[0], fresh, chosen)
    q_all = lax.all_to_all(q_blocks, SEQ, 0, 0, tiled=True)
    swap = [(position(z, x, c), position(z, x, 1 - c)) for z in range(4) for x in range(4) for c in range(2)]
    first = lax.ppermute(send, SEQ, swap)
    stacked = call(stack_kernel, [shape((2, 2, tokens, BLOCK), bf16)] * 4, n_in=2)(keep, first)
    others = [lax.ppermute(stacked[k], SEQ, ring_pairs(k)) for k in (1, 2, 3)]

    rows = 32 * SLOT_PAD
    scratch = [pltpu.VMEM((4 * tokens, BLOCK), bf16), pltpu.VMEM((HEADS_HERE, HEAD_DIM, 4 * tokens), bf16)]
    mixed, stats = call(
        attention_first_kernel,
        [shape((HEADS_HERE, HEAD_DIM, rows), f32), shape((8, rows), f32)],
        scratch=scratch,
        n_in=3,
        limit=24,
        us=2.8,
    )(q_all, stacked[0], others[0])
    partial = call(
        attention_second_kernel,
        shape((32, SLOT_PAD, BLOCK), bf16),
        scratch=scratch,
        n_in=5,
        limit=24,
        us=3.0,
    )(q_all, others[1], others[2], mixed, stats)
    parts = lax.all_to_all(partial, SEQ, 0, 0, tiled=True)
    rows, mod = load(partial, [rows_in, modulation], 16)
    hidden, normed, mark = call(
        combine_kernel,
        [shape((slots, width), f32), shape((2 * slots, width // 2), bf16), shape((16, 128), bf16)],
        scratch=[pltpu.VMEM((128, 128), f32), pltpu.VMEM((128, 128), f32)],
        n_in=3,
        us=1.6,
    )(parts, rows, mod)

    far, near, last = (lax.ppermute(normed, "y", turn(k)) for k in (2, 1, 3))
    visits = [near, far, last]
    up, down = load(mark, [w_up, w_down], 34)
    terms = call(
        feed_kernel,
        [shape((2 * slots, width // 2), bf16)] * 4,
        scratch=[
            pltpu.VMEM((4 * SLOT_PAD, width), bf16),
            pltpu.VMEM((4 * SLOT_PAD, w_up.shape[1]), bf16),
            pltpu.VMEM((4 * SLOT_PAD, width), f32),
        ],
        n_in=7,
        us=3.7,
    )(normed, *visits, up, b_up[None], down)
    back = [lax.ppermute(terms[k], "y", turn(-k)) for k in (2, 1, 3)]
    return call(finish_kernel, shape((1, slots, width), bf16), n_in=8, smem=(0,), us=1.4)(
        counts, terms[0], *back, hidden, modulation, b_down[None]
    )


def solution(mesh):
    whole = jax.sharding.Mesh(mesh.devices.reshape(4, 4, 4, 2), ("y", "z", "x", "core"))
    placed = (
        P("y", SEQ, None),
        P("y", SEQ, None, None),
        P("y", SEQ, None, None),
        P("y", SEQ),
        P("y", SEQ),
        P("y", None, None),
        P(None, "y"),
        P("y"),
        P("y", None),
        P(),
    )
    return jax.shard_map(body, mesh=whole, in_specs=placed, out_specs=P("y", SEQ, None), check_vma=False)
```

```python
import jax
import jax.numpy as jnp
from jax import lax
from jax.experimental import pallas as pl
from jax.experimental.pallas import tpu as pltpu
from jax.sharding import PartitionSpec as P

HEAD_DIM = 128
HEADS_HERE = 3
BLOCK = HEADS_HERE * HEAD_DIM
SLOT_PAD = 32
LOG2E = 1.4426950408889634
EPS = 1e-06
SEQ = ("z", "x", "core")
bf16 = jnp.bfloat16
f32 = jnp.float32
i32 = jnp.int32
MB = 1 << 20


def call(kernel, out_shape, scratch=(), limit=16, smem=(), hbm=(), n_in=None, us=1.0):
    def space(i):
        return pltpu.SMEM if i in smem else pltpu.HBM if i in hbm else pltpu.VMEM

    return pl.pallas_call(
        kernel,
        out_shape=out_shape,
        in_specs=[pl.BlockSpec(memory_space=space(i)) for i in range(n_in)],
        scratch_shapes=list(scratch),
        compiler_params=pltpu.CompilerParams(vmem_limit_bytes=limit * MB),
        cost_estimate=pl.CostEstimate(flops=0, transcendentals=0, bytes_accessed=int(us * 3.3e6)),
    )


def fetch(pairs, sems):
    copies = [pltpu.make_async_copy(src, dst, sems.at[i]) for i, (src, dst) in enumerate(pairs)]
    for copy in copies:
        copy.start()
    for copy in copies:
        copy.wait()


def pack_kernel(
    count_ref, kv_hbm, fresh_hbm, chosen_hbm, q_hbm, keep_hbm, send_hbm,
    kv_ref, fresh_ref, chosen_ref, patched, q_out, in_sems, out_sems,
):
    sources = [
        (fresh_hbm.at[0], fresh_ref.at[0]),
        (kv_hbm, kv_ref),
        (fresh_hbm.at[1:3], fresh_ref.at[1:3]),
        (chosen_hbm, chosen_ref),
    ]
    copies = [pltpu.make_async_copy(src, dst, in_sems.at[i]) for i, (src, dst) in enumerate(sources)]
    for copy in copies:
        copy.start()
    tokens = kv_ref.shape[0]
    slots = fresh_ref.shape[1]
    copies[0].wait()
    for dest in range(32):
        z, x, core = dest // 8, dest // 2 % 4, dest % 2
        group = x if core == 0 else 4 + z
        q_out[dest, :slots, :] = fresh_ref[0, :, group * BLOCK : (group + 1) * BLOCK]
        q_out[dest, slots:, :] = jnp.zeros((SLOT_PAD - slots, BLOCK), bf16)
    outs = [pltpu.make_async_copy(q_out, q_hbm, out_sems.at[0])]
    outs[0].start()

    core, ring_x, ring_z = (lax.axis_index(a) for a in ("core", "x", "z"))
    count = count_ref[0, 0]
    for copy in copies[1:]:
        copy.wait()
    token_id = lax.broadcasted_iota(i32, (tokens, slots), 0)
    slot_id = lax.broadcasted_iota(i32, (tokens, slots), 1)
    hit = (token_id == chosen_ref[...]) & (slot_id < count)
    hot = jnp.where(hit, 1.0, 0.0)
    taken = jnp.sum(hot, axis=1, keepdims=True) > 0.5
    hot = hot.astype(bf16)
    old = jnp.swapaxes(kv_ref[...], 0, 1)
    half = 4 * BLOCK
    for which in range(2):
        new = jnp.dot(hot, fresh_ref[1 + which], preferred_element_type=f32)
        patched[which] = jnp.where(taken, new, old[which].astype(f32)).astype(bf16)
        for k in range(4):
            mine = lax.rem(jnp.where(core == 0, ring_x, ring_z) + k, 4)
            other = lax.rem(jnp.where(core == 0, ring_z, ring_x) + k, 4)
            at_mine = pl.multiple_of(core * half + mine * BLOCK, BLOCK)
            at_other = pl.multiple_of((1 - core) * half + other * BLOCK, BLOCK)
            for at, target in ((at_other, send_hbm), (at_mine, keep_hbm)):
                copy = pltpu.make_async_copy(
                    patched.at[which, :, pl.ds(at, BLOCK)], target.at[k, which], out_sems.at[len(outs)]
                )
                copy.start()
                outs.append(copy)
    for copy in outs:
        copy.wait()


def stack_kernel(keep_ref, first_ref, *out_refs):
    for k, out_ref in enumerate(out_refs):
        out_ref[0] = keep_ref[k]
        out_ref[1] = first_ref[k]


def gather_keys(sources, keys, values_t):
    rows = 128
    at = 0
    for ref in sources:
        for core in range(2):
            keys[at : at + rows, :] = ref[core, 0]
            for h in range(HEADS_HERE):
                cols = slice(h * HEAD_DIM, (h + 1) * HEAD_DIM)
                values_t[h, :, at : at + rows] = ref[core, 1, :, cols].T
            at += rows


def head_scores(q_all, keys, h):
    cols = slice(h * HEAD_DIM, (h + 1) * HEAD_DIM)
    return lax.dot_general(
        keys[:, cols], q_all[:, cols], (((1,), (1,)), ((), ())), preferred_element_type=f32
    )


SCALE = LOG2E * HEAD_DIM**-0.5


def attention_first_kernel(q_ref, r0_ref, mixed_ref, stats_ref, keys, values_t):
    gather_keys((r0_ref,), keys, values_t)
    q_all = q_ref[...].reshape(-1, BLOCK)
    for h in range(HEADS_HERE):
        scores = head_scores(q_all, keys, h)
        top = jnp.max(scores, axis=0, keepdims=True)
        weights = jnp.exp2((scores - top) * SCALE)
        stats_ref[h : h + 1, :] = top
        stats_ref[4 + h : 5 + h, :] = jnp.sum(weights, axis=0, keepdims=True)
        mixed_ref[h] = jnp.dot(values_t[h], weights.astype(bf16), preferred_element_type=f32)


def attention_second_kernel(
    q_ref, r1_ref, r2_ref, r3_ref, mixed_ref, stats_ref, after_ref, out_ref, keys, values_t
):
    gather_keys((r1_ref, r2_ref, r3_ref), keys, values_t)
    q_all = q_ref[...].reshape(-1, BLOCK)
    for h in range(HEADS_HERE):
        cols = slice(h * HEAD_DIM, (h + 1) * HEAD_DIM)
        scores = head_scores(q_all, keys, h)
        before = stats_ref[h : h + 1, :]
        top = jnp.maximum(jnp.max(scores, axis=0, keepdims=True), before)
        weights = jnp.exp2((scores - top) * SCALE)
        shrink = jnp.exp2((before - top) * SCALE)
        mass = jnp.sum(weights, axis=0, keepdims=True) + shrink * stats_ref[4 + h : 5 + h, :]
        mixed = jnp.dot(values_t[h], weights.astype(bf16), preferred_element_type=f32)
        mixed = (mixed + shrink * mixed_ref[h]) * (1.0 / mass)
        level = top * SCALE + jnp.log2(mass)
        p0 = level.astype(bf16).astype(f32)
        rest = level - p0
        p1 = rest.astype(bf16).astype(f32)
        p2 = rest - p1
        for g in range(q_all.shape[0] // 128):
            lanes = slice(g * 128, (g + 1) * 128)
            turned = mixed[:, lanes].T
            row = lax.broadcasted_iota(i32, (128, HEAD_DIM), 0) % SLOT_PAD
            turned = jnp.where(row == 28, p0[:, lanes], turned)
            turned = jnp.where(row == 29, p1[:, lanes], turned)
            turned = jnp.where(row == 30, p2[:, lanes], turned)
            out_ref[g * 4 : (g + 1) * 4, :, cols] = turned.astype(bf16).reshape(4, SLOT_PAD, HEAD_DIM)


def fold(rows):
    half = rows.shape[1] // 2
    return jnp.concatenate([rows[:, :half], rows[:, half:]], axis=0)


def unfold(folded):
    count = folded.shape[0] // 2
    return jnp.concatenate([folded[:count], folded[count:]], axis=1)


def combine_kernel(parts_ref, rows_ref, mod_ref, hidden_ref, normed_ref, mark_ref, levels, turned):
    slots = rows_ref.shape[1]
    place = 2 * lax.rem(lax.axis_index("x"), 2) + lax.axis_index("core")
    heads = 24

    def source(part, group):
        return part * 8 + group * 2 if group < 4 else (group - 4) * 8 + part * 2 + 1

    for part in range(4):
        for group in range(8):
            tail = parts_ref[source(part, group), 24:32, :].astype(f32)
            level = tail[4:5] + tail[5:6] + tail[6:7]
            for h in range(HEADS_HERE):
                at = part * heads + group * HEADS_HERE + h
                levels[at : at + 1, :] = level[:, h * HEAD_DIM : (h + 1) * HEAD_DIM]
    pieces = [levels[p * heads : (p + 1) * heads, :] for p in range(4)]
    top = jnp.maximum(jnp.maximum(pieces[0], pieces[1]), jnp.maximum(pieces[2], pieces[3]))
    weights = [jnp.exp2(piece - top) for piece in pieces]
    total = 1.0 / (weights[0] + weights[1] + weights[2] + weights[3])
    for p in range(4):
        levels[p * heads : (p + 1) * heads, :] = weights[p] * total
    levels[4 * heads :, :] = jnp.zeros((128 - 4 * heads, 128), f32)
    turned[...] = levels[...].T
    mine = turned[pl.ds(pl.multiple_of(place * SLOT_PAD, SLOT_PAD), SLOT_PAD), :]
    shifts = mod_ref[0].astype(f32)
    for group in range(8):
        for h in range(HEADS_HERE):
            head = group * HEADS_HERE + h
            acc = jnp.zeros((SLOT_PAD, HEAD_DIM), f32)
            for part in range(4):
                column = part * heads + head
                block = parts_ref[source(part, group), :, h * HEAD_DIM : (h + 1) * HEAD_DIM]
                acc = acc + mine[:, column : column + 1] * block.astype(f32)
            cols = slice(head * HEAD_DIM, (head + 1) * HEAD_DIM)
            attended = acc[:slots] * shifts[2:3, cols]
            hidden_ref[:, cols] = rows_ref[0, :, cols].astype(f32) + attended
    hidden = hidden_ref[...]
    center = hidden - jnp.mean(hidden, axis=1, keepdims=True)
    spread = jnp.mean(center * center, axis=1, keepdims=True)
    normed = center * lax.rsqrt(spread + EPS) * (1.0 + shifts[1:2]) + shifts[0:1]
    normed_ref[...] = fold(normed).astype(bf16)
    mark_ref[...] = jnp.zeros(mark_ref.shape, bf16)


def load_kernel(after_ref, *refs):
    count = len(refs) // 2
    fetch(list(zip(refs[:count], refs[count : 2 * count])), refs[2 * count])


def load(after, arrays, limit):
    return call(
        load_kernel,
        [jax.ShapeDtypeStruct(v.shape, bf16) for v in arrays],
        scratch=[pltpu.SemaphoreType.DMA((len(arrays),))],
        n_in=1 + len(arrays),
        hbm=range(1 + len(arrays)),
        limit=limit,
        us=3.6,
    )(after, *arrays)


def feed_kernel(
    r0_ref, r1_ref, r2_ref, r3_ref, up_ref, b_up_ref, down_ref, o0, o1, o2, o3, rows_ref, active, terms
):
    chunk = 512
    slots = r0_ref.shape[0] // 2
    none = jnp.zeros((SLOT_PAD - slots, rows_ref.shape[1]), f32)
    for i, ref in enumerate((r0_ref, r1_ref, r2_ref, r3_ref)):
        block = jnp.concatenate([unfold(ref[...].astype(f32)), none], axis=0)
        rows_ref[i * SLOT_PAD : (i + 1) * SLOT_PAD, :] = block.astype(bf16)
    rows = rows_ref[...]
    for start in range(0, up_ref.shape[1], chunk):
        cols = slice(start, start + chunk)
        lifted = jnp.dot(rows, up_ref[:, cols], preferred_element_type=f32)
        lifted = lifted + b_up_ref[:, cols].astype(f32)
        active[:, cols] = jax.nn.gelu(lifted, approximate=True).astype(bf16)
    for start in range(0, down_ref.shape[1], chunk):
        cols = slice(start, start + chunk)
        terms[:, cols] = jnp.dot(active[...], down_ref[:, cols], preferred_element_type=f32)
    for i, out_ref in enumerate((o0, o1, o2, o3)):
        out_ref[...] = fold(terms[i * SLOT_PAD : i * SLOT_PAD + slots, :]).astype(bf16)


def finish_kernel(count_ref, t0_ref, t1_ref, t2_ref, t3_ref, hidden_ref, mod_ref, b_down_ref, out_ref):
    total = t0_ref[...].astype(f32)
    for ref in (t1_ref, t2_ref, t3_ref):
        total = total + ref[...].astype(f32)
    feed_out = unfold(total) + b_down_ref[...].astype(f32)
    result = hidden_ref[...] + mod_ref[0, 3:4].astype(f32) * feed_out
    live = lax.broadcasted_iota(i32, result.shape, 0) < count_ref[0, 0]
    out_ref[0] = jnp.where(live, result, 0.0).astype(bf16)


def position(z, x, core):
    return (z % 4) * 8 + (x % 4) * 2 + core


def ring_pairs(k):
    return [
        (position(z, x, c), position(z, x + k, 0) if c == 0 else position(z + k, x, 1))
        for z in range(4)
        for x in range(4)
        for c in range(2)
    ]


def turn(k):
    return [(y, (y + k) % 4) for y in range(4)]


def body(rows_in, fresh_qkv, kv_cache, chosen, counts, modulation, w_up, b_up, w_down, b_down):
    shape = jax.ShapeDtypeStruct
    slots, width = rows_in.shape[1], rows_in.shape[2]
    tokens = kv_cache.shape[1]
    fresh = jnp.swapaxes(fresh_qkv[0], 0, 1)
    q_blocks, keep, send = pl.pallas_call(
        pack_kernel,
        out_shape=[shape((32, SLOT_PAD, BLOCK), bf16)] + [shape((4, 2, tokens, BLOCK), bf16)] * 2,
        in_specs=[pl.BlockSpec(memory_space=pltpu.SMEM)] + [pl.BlockSpec(memory_space=pltpu.HBM)] * 3,
        out_specs=[pl.BlockSpec(memory_space=pltpu.HBM)] * 3,
        scratch_shapes=[
            pltpu.VMEM((tokens, 2, width), bf16),
            pltpu.VMEM((3, slots, width), bf16),
            pltpu.VMEM((1, slots), i32),
            pltpu.VMEM((2, tokens, width), bf16),
            pltpu.VMEM((32, SLOT_PAD, BLOCK), bf16),
            pltpu.SemaphoreType.DMA((4,)),
            pltpu.SemaphoreType.DMA((17,)),
        ],
        compiler_params=pltpu.CompilerParams(vmem_limit_bytes=61 * MB),
    )(counts, kv_cache[0], fresh, chosen)
    q_all = lax.all_to_all(q_blocks, SEQ, 0, 0, tiled=True)
    swap = [(position(z, x, c), position(z, x, 1 - c)) for z in range(4) for x in range(4) for c in range(2)]
    first = lax.ppermute(send, SEQ, swap)
    stacked = call(stack_kernel, [shape((2, 2, tokens, BLOCK), bf16)] * 4, n_in=2)(keep, first)
    others = [lax.ppermute(stacked[k], SEQ, ring_pairs(k)) for k in (1, 2, 3)]


    def key_scratch(count):
        return [pltpu.VMEM((count, BLOCK), bf16), pltpu.VMEM((HEADS_HERE, HEAD_DIM, count), bf16)]

    mixed, stats = call(
        attention_first_kernel,
        [shape((HEADS_HERE, HEAD_DIM, 32 * SLOT_PAD), f32), shape((8, 32 * SLOT_PAD), f32)],
        scratch=key_scratch(2 * tokens),
        n_in=2,
        limit=24,
        us=1.6,
    )(q_all, stacked[0])
    rows, mod = load(stats, [rows_in, modulation], 16)
    partial = call(
        attention_second_kernel,
        shape((32, SLOT_PAD, BLOCK), bf16),
        scratch=key_scratch(6 * tokens),
        n_in=7,
        limit=24,
        us=4.6,
    )(q_all, *others, mixed, stats, mod)
    parts = lax.all_to_all(partial, SEQ, 0, 0, tiled=True)
    hidden, normed, mark = call(
        combine_kernel,
        [shape((slots, width), f32), shape((2 * slots, width // 2), bf16), shape((16, 128), bf16)],
        scratch=[pltpu.VMEM((128, 128), f32), pltpu.VMEM((128, 128), f32)],
        n_in=3,
        us=1.6,
    )(parts, rows, mod)

    far, near, last = (lax.ppermute(normed, "y", turn(k)) for k in (2, 1, 3))
    visits = [near, far, last]
    up, down = load(mark, [w_up, w_down], 34)
    terms = call(
        feed_kernel,
        [shape((2 * slots, width // 2), bf16)] * 4,
        scratch=[
            pltpu.VMEM((4 * SLOT_PAD, width), bf16),
            pltpu.VMEM((4 * SLOT_PAD, w_up.shape[1]), bf16),
            pltpu.VMEM((4 * SLOT_PAD, width), f32),
        ],
        n_in=7,
        us=3.7,
    )(normed, *visits, up, b_up[None], down)
    back = [lax.ppermute(terms[k], "y", turn(-k)) for k in (2, 1, 3)]
    return call(finish_kernel, shape((1, slots, width), bf16), n_in=8, smem=(0,), us=1.4)(
        counts, terms[0], *back, hidden, modulation, b_down[None]
    )


def solution(mesh):
    whole = jax.sharding.Mesh(mesh.devices.reshape(4, 4, 4, 2), ("y", "z", "x", "core"))
    placed = (
        P("y", SEQ, None),
        P("y", SEQ, None, None),
        P("y", SEQ, None, None),
        P("y", SEQ),
        P("y", SEQ),
        P("y", None, None),
        P(None, "y"),
        P("y"),
        P("y", None),
        P(),
    )
    return jax.shard_map(body, mesh=whole, in_specs=placed, out_specs=P("y", SEQ, None), check_vma=False)
```

```python
import jax
import jax.numpy as jnp
from jax import lax
from jax.experimental import pallas as pl
from jax.experimental.pallas import tpu as pltpu
from jax.sharding import PartitionSpec as P

HEAD_DIM = 128
HEADS_HERE = 3
BLOCK = HEADS_HERE * HEAD_DIM
SLOT_PAD = 32
LOG2E = 1.4426950408889634
EPS = 1e-06
SEQ = ("z", "x", "core")
bf16 = jnp.bfloat16
f32 = jnp.float32
i32 = jnp.int32
MB = 1 << 20


def call(kernel, out_shape, scratch=(), limit=16, smem=(), hbm=(), n_in=None, us=1.0):
    def space(i):
        return pltpu.SMEM if i in smem else pltpu.HBM if i in hbm else pltpu.VMEM

    return pl.pallas_call(
        kernel,
        out_shape=out_shape,
        in_specs=[pl.BlockSpec(memory_space=space(i)) for i in range(n_in)],
        scratch_shapes=list(scratch),
        compiler_params=pltpu.CompilerParams(vmem_limit_bytes=limit * MB),
        cost_estimate=pl.CostEstimate(flops=0, transcendentals=0, bytes_accessed=int(us * 3.3e6)),
    )


def fetch(pairs, sems):
    copies = [pltpu.make_async_copy(src, dst, sems.at[i]) for i, (src, dst) in enumerate(pairs)]
    for copy in copies:
        copy.start()
    for copy in copies:
        copy.wait()


def pack_kernel(
    count_ref, kv_hbm, fresh_hbm, chosen_hbm, q_hbm, keep_hbm, send_hbm,
    kv_ref, fresh_ref, chosen_ref, patched, q_out, in_sems, out_sems,
):
    sources = [
        (fresh_hbm.at[0], fresh_ref.at[0]),
        (fresh_hbm.at[1:3], fresh_ref.at[1:3]),
        (chosen_hbm, chosen_ref),
        (kv_hbm.at[0:64], kv_ref.at[0:64]),
        (kv_hbm.at[64:128], kv_ref.at[64:128]),
    ]
    copies = [pltpu.make_async_copy(src, dst, in_sems.at[i]) for i, (src, dst) in enumerate(sources)]
    for copy in copies:
        copy.start()
    tokens = kv_ref.shape[0]
    slots = fresh_ref.shape[1]
    copies[0].wait()
    for dest in range(32):
        z, x, core = dest // 8, dest // 2 % 4, dest % 2
        group = x if core == 0 else 4 + z
        q_out[dest, :slots, :] = fresh_ref[0, :, group * BLOCK : (group + 1) * BLOCK]
        q_out[dest, slots:, :] = jnp.zeros((SLOT_PAD - slots, BLOCK), bf16)
    outs = [pltpu.make_async_copy(q_out, q_hbm, out_sems.at[0])]
    outs[0].start()

    core, ring_x, ring_z = (lax.axis_index(a) for a in ("core", "x", "z"))
    count = count_ref[0, 0]
    copies[1].wait()
    copies[2].wait()
    token_id = lax.broadcasted_iota(i32, (tokens, slots), 0)
    slot_id = lax.broadcasted_iota(i32, (tokens, slots), 1)
    hit = (token_id == chosen_ref[...]) & (slot_id < count)
    hot = jnp.where(hit, 1.0, 0.0)
    taken = jnp.sum(hot, axis=1, keepdims=True) > 0.5
    hot = hot.astype(bf16)
    half = 4 * BLOCK
    part = tokens // 2
    for step in range(2):
        here = slice(step * part, (step + 1) * part)
        copies[3 + step].wait()
        old = jnp.swapaxes(kv_ref[here], 0, 1)
        for which in range(2):
            new = jnp.dot(hot[here], fresh_ref[1 + which], preferred_element_type=f32)
            patched[which, here] = jnp.where(taken[here], new, old[which].astype(f32)).astype(bf16)
            for k in range(4):
                mine = lax.rem(jnp.where(core == 0, ring_x, ring_z) + k, 4)
                other = lax.rem(jnp.where(core == 0, ring_z, ring_x) + k, 4)
                at_mine = pl.multiple_of(core * half + mine * BLOCK, BLOCK)
                at_other = pl.multiple_of((1 - core) * half + other * BLOCK, BLOCK)
                for at, target in ((at_other, send_hbm), (at_mine, keep_hbm)):
                    copy = pltpu.make_async_copy(
                        patched.at[which, here, pl.ds(at, BLOCK)],
                        target.at[k, which, here],
                        out_sems.at[len(outs)],
                    )
                    copy.start()
                    outs.append(copy)
    for copy in outs:
        copy.wait()


def stack_kernel(keep_ref, first_ref, *out_refs):
    for k, out_ref in enumerate(out_refs, 1):
        out_ref[0] = keep_ref[k]
        out_ref[1] = first_ref[k]


def gather_keys(sources, keys, values_t):
    rows = 128
    at = 0
    for ref in sources:
        keys[at : at + rows, :] = ref[0]
        for h in range(HEADS_HERE):
            cols = slice(h * HEAD_DIM, (h + 1) * HEAD_DIM)
            values_t[h, :, at : at + rows] = ref[1, :, cols].T
        at += rows


def head_scores(q_all, keys, h):
    cols = slice(h * HEAD_DIM, (h + 1) * HEAD_DIM)
    return lax.dot_general(
        keys[:, cols], q_all[:, cols], (((1,), (1,)), ((), ())), preferred_element_type=f32
    )


SCALE = LOG2E * HEAD_DIM**-0.5


def attention_first_kernel(q_ref, keep_ref, first_ref, mixed_ref, stats_ref, keys, values_t):
    gather_keys((keep_ref.at[0], first_ref.at[0]), keys, values_t)
    q_all = q_ref[...].reshape(-1, BLOCK)
    for h in range(HEADS_HERE):
        scores = head_scores(q_all, keys, h)
        top = jnp.max(scores, axis=0, keepdims=True)
        weights = jnp.exp2((scores - top) * SCALE)
        stats_ref[h : h + 1, :] = top
        stats_ref[4 + h : 5 + h, :] = jnp.sum(weights, axis=0, keepdims=True)
        mixed_ref[h] = jnp.dot(values_t[h], weights.astype(bf16), preferred_element_type=f32)


def attention_second_kernel(
    q_ref, r1_ref, r2_ref, r3_ref, mixed_ref, stats_ref, after_ref, out_ref, keys, values_t
):
    sources = [ref.at[core] for ref in (r1_ref, r2_ref, r3_ref) for core in range(2)]
    gather_keys(sources, keys, values_t)
    q_all = q_ref[...].reshape(-1, BLOCK)
    for h in range(HEADS_HERE):
        cols = slice(h * HEAD_DIM, (h + 1) * HEAD_DIM)
        scores = head_scores(q_all, keys, h)
        before = stats_ref[h : h + 1, :]
        top = jnp.maximum(jnp.max(scores, axis=0, keepdims=True), before)
        weights = jnp.exp2((scores - top) * SCALE)
        shrink = jnp.exp2((before - top) * SCALE)
        mass = jnp.sum(weights, axis=0, keepdims=True) + shrink * stats_ref[4 + h : 5 + h, :]
        mixed = jnp.dot(values_t[h], weights.astype(bf16), preferred_element_type=f32)
        mixed = (mixed + shrink * mixed_ref[h]) * (1.0 / mass)
        level = top * SCALE + jnp.log2(mass)
        p0 = level.astype(bf16).astype(f32)
        rest = level - p0
        p1 = rest.astype(bf16).astype(f32)
        p2 = rest - p1
        for g in range(q_all.shape[0] // 128):
            lanes = slice(g * 128, (g + 1) * 128)
            turned = mixed[:, lanes].T
            row = lax.broadcasted_iota(i32, (128, HEAD_DIM), 0) % SLOT_PAD
            turned = jnp.where(row == 28, p0[:, lanes], turned)
            turned = jnp.where(row == 29, p1[:, lanes], turned)
            turned = jnp.where(row == 30, p2[:, lanes], turned)
            out_ref[g * 4 : (g + 1) * 4, :, cols] = turned.astype(bf16).reshape(4, SLOT_PAD, HEAD_DIM)


def fold(rows):
    half = rows.shape[1] // 2
    return jnp.concatenate([rows[:, :half], rows[:, half:]], axis=0)


def unfold(folded):
    count = folded.shape[0] // 2
    return jnp.concatenate([folded[:count], folded[count:]], axis=1)


def combine_kernel(parts_ref, rows_ref, mod_ref, hidden_ref, normed_ref, mark_ref, levels, turned):
    slots = rows_ref.shape[1]
    place = 2 * lax.rem(lax.axis_index("x"), 2) + lax.axis_index("core")
    heads = 24

    def source(part, group):
        return part * 8 + group * 2 if group < 4 else (group - 4) * 8 + part * 2 + 1

    for part in range(4):
        for group in range(8):
            tail = parts_ref[source(part, group), 24:32, :].astype(f32)
            level = tail[4:5] + tail[5:6] + tail[6:7]
            for h in range(HEADS_HERE):
                at = part * heads + group * HEADS_HERE + h
                levels[at : at + 1, :] = level[:, h * HEAD_DIM : (h + 1) * HEAD_DIM]
    pieces = [levels[p * heads : (p + 1) * heads, :] for p in range(4)]
    top = jnp.maximum(jnp.maximum(pieces[0], pieces[1]), jnp.maximum(pieces[2], pieces[3]))
    weights = [jnp.exp2(piece - top) for piece in pieces]
    total = 1.0 / (weights[0] + weights[1] + weights[2] + weights[3])
    for p in range(4):
        levels[p * heads : (p + 1) * heads, :] = weights[p] * total
    levels[4 * heads :, :] = jnp.zeros((128 - 4 * heads, 128), f32)
    turned[...] = levels[...].T
    mine = turned[pl.ds(pl.multiple_of(place * SLOT_PAD, SLOT_PAD), SLOT_PAD), :]
    shifts = mod_ref[0].astype(f32)
    for group in range(8):
        for h in range(HEADS_HERE):
            head = group * HEADS_HERE + h
            acc = jnp.zeros((SLOT_PAD, HEAD_DIM), f32)
            for part in range(4):
                column = part * heads + head
                block = parts_ref[source(part, group), :, h * HEAD_DIM : (h + 1) * HEAD_DIM]
                acc = acc + mine[:, column : column + 1] * block.astype(f32)
            cols = slice(head * HEAD_DIM, (head + 1) * HEAD_DIM)
            attended = acc[:slots] * shifts[2:3, cols]
            hidden_ref[:, cols] = rows_ref[0, :, cols].astype(f32) + attended
    hidden = hidden_ref[...]
    center = hidden - jnp.mean(hidden, axis=1, keepdims=True)
    spread = jnp.mean(center * center, axis=1, keepdims=True)
    normed = center * lax.rsqrt(spread + EPS) * (1.0 + shifts[1:2]) + shifts[0:1]
    normed_ref[...] = fold(normed).astype(bf16)
    mark_ref[...] = jnp.zeros(mark_ref.shape, bf16)


def load_kernel(after_ref, *refs):
    count = len(refs) // 2
    fetch(list(zip(refs[:count], refs[count : 2 * count])), refs[2 * count])


def load(after, arrays, limit):
    return call(
        load_kernel,
        [jax.ShapeDtypeStruct(v.shape, bf16) for v in arrays],
        scratch=[pltpu.SemaphoreType.DMA((len(arrays),))],
        n_in=1 + len(arrays),
        hbm=range(1 + len(arrays)),
        limit=limit,
        us=3.6,
    )(after, *arrays)


def feed_kernel(
    r0_ref, r1_ref, r2_ref, r3_ref, up_ref, b_up_ref, down_ref, o0, o1, o2, o3, rows_ref, active, terms
):
    chunk = 512
    slots = r0_ref.shape[0] // 2
    none = jnp.zeros((SLOT_PAD - slots, rows_ref.shape[1]), f32)
    for i, ref in enumerate((r0_ref, r1_ref, r2_ref, r3_ref)):
        block = jnp.concatenate([unfold(ref[...].astype(f32)), none], axis=0)
        rows_ref[i * SLOT_PAD : (i + 1) * SLOT_PAD, :] = block.astype(bf16)
    rows = rows_ref[...]
    for start in range(0, up_ref.shape[1], chunk):
        cols = slice(start, start + chunk)
        lifted = jnp.dot(rows, up_ref[:, cols], preferred_element_type=f32)
        lifted = lifted + b_up_ref[:, cols].astype(f32)
        active[:, cols] = jax.nn.gelu(lifted, approximate=True).astype(bf16)
    for start in range(0, down_ref.shape[1], chunk):
        cols = slice(start, start + chunk)
        terms[:, cols] = jnp.dot(active[...], down_ref[:, cols], preferred_element_type=f32)
    for i, out_ref in enumerate((o0, o1, o2, o3)):
        out_ref[...] = fold(terms[i * SLOT_PAD : i * SLOT_PAD + slots, :]).astype(bf16)


def finish_kernel(count_ref, t0_ref, t1_ref, t2_ref, t3_ref, hidden_ref, mod_ref, b_down_ref, out_ref):
    total = t0_ref[...].astype(f32)
    for ref in (t1_ref, t2_ref, t3_ref):
        total = total + ref[...].astype(f32)
    feed_out = unfold(total) + b_down_ref[...].astype(f32)
    result = hidden_ref[...] + mod_ref[0, 3:4].astype(f32) * feed_out
    live = lax.broadcasted_iota(i32, result.shape, 0) < count_ref[0, 0]
    out_ref[0] = jnp.where(live, result, 0.0).astype(bf16)


def position(z, x, core):
    return (z % 4) * 8 + (x % 4) * 2 + core


def ring_pairs(k):
    return [
        (position(z, x, c), position(z, x + k, 0) if c == 0 else position(z + k, x, 1))
        for z in range(4)
        for x in range(4)
        for c in range(2)
    ]


def turn(k):
    return [(y, (y + k) % 4) for y in range(4)]


def body(rows_in, fresh_qkv, kv_cache, chosen, counts, modulation, w_up, b_up, w_down, b_down):
    shape = jax.ShapeDtypeStruct
    slots, width = rows_in.shape[1], rows_in.shape[2]
    tokens = kv_cache.shape[1]
    fresh = jnp.swapaxes(fresh_qkv[0], 0, 1)
    q_blocks, keep, send = pl.pallas_call(
        pack_kernel,
        out_shape=[shape((32, SLOT_PAD, BLOCK), bf16)] + [shape((4, 2, tokens, BLOCK), bf16)] * 2,
        in_specs=[pl.BlockSpec(memory_space=pltpu.SMEM)] + [pl.BlockSpec(memory_space=pltpu.HBM)] * 3,
        out_specs=[pl.BlockSpec(memory_space=pltpu.HBM)] * 3,
        scratch_shapes=[
            pltpu.VMEM((tokens, 2, width), bf16),
            pltpu.VMEM((3, slots, width), bf16),
            pltpu.VMEM((1, slots), i32),
            pltpu.VMEM((2, tokens, width), bf16),
            pltpu.VMEM((32, SLOT_PAD, BLOCK), bf16),
            pltpu.SemaphoreType.DMA((5,)),
            pltpu.SemaphoreType.DMA((33,)),
        ],
        compiler_params=pltpu.CompilerParams(vmem_limit_bytes=61 * MB),
    )(counts, kv_cache[0], fresh, chosen)
    q_all = lax.all_to_all(q_blocks, SEQ, 0, 0, tiled=True)
    swap = [(position(z, x, c), position(z, x, 1 - c)) for z in range(4) for x in range(4) for c in range(2)]
    first = lax.ppermute(send, SEQ, swap)
    stacked = call(stack_kernel, [shape((2, 2, tokens, BLOCK), bf16)] * 3, n_in=2)(keep, first)
    others = [lax.ppermute(stacked[k - 1], SEQ, ring_pairs(k)) for k in (1, 2, 3)]


    def key_scratch(count):
        return [pltpu.VMEM((count, BLOCK), bf16), pltpu.VMEM((HEADS_HERE, HEAD_DIM, count), bf16)]

    mixed, stats = call(
        attention_first_kernel,
        [shape((HEADS_HERE, HEAD_DIM, 32 * SLOT_PAD), f32), shape((8, 32 * SLOT_PAD), f32)],
        scratch=key_scratch(2 * tokens),
        n_in=3,
        limit=24,
        us=1.6,
    )(q_all, keep, first)
    rows, mod = load(stats, [rows_in, modulation], 16)
    partial = call(
        attention_second_kernel,
        shape((32, SLOT_PAD, BLOCK), bf16),
        scratch=key_scratch(6 * tokens),
        n_in=7,
        limit=24,
        us=4.6,
    )(q_all, *others, mixed, stats, mod)
    parts = lax.all_to_all(partial, SEQ, 0, 0, tiled=True)
    hidden, normed, mark = call(
        combine_kernel,
        [shape((slots, width), f32), shape((2 * slots, width // 2), bf16), shape((16, 128), bf16)],
        scratch=[pltpu.VMEM((128, 128), f32), pltpu.VMEM((128, 128), f32)],
        n_in=3,
        us=1.6,
    )(parts, rows, mod)

    far, near, last = (lax.ppermute(normed, "y", turn(k)) for k in (2, 1, 3))
    visits = [near, far, last]
    up, down = load(mark, [w_up, w_down], 34)
    terms = call(
        feed_kernel,
        [shape((2 * slots, width // 2), bf16)] * 4,
        scratch=[
            pltpu.VMEM((4 * SLOT_PAD, width), bf16),
            pltpu.VMEM((4 * SLOT_PAD, w_up.shape[1]), bf16),
            pltpu.VMEM((4 * SLOT_PAD, width), f32),
        ],
        n_in=7,
        us=3.7,
    )(normed, *visits, up, b_up[None], down)
    back = [lax.ppermute(terms[k], "y", turn(-k)) for k in (2, 1, 3)]
    return call(finish_kernel, shape((1, slots, width), bf16), n_in=8, smem=(0,), us=1.4)(
        counts, terms[0], *back, hidden, modulation, b_down[None]
    )


def solution(mesh):
    whole = jax.sharding.Mesh(mesh.devices.reshape(4, 4, 4, 2), ("y", "z", "x", "core"))
    placed = (
        P("y", SEQ, None),
        P("y", SEQ, None, None),
        P("y", SEQ, None, None),
        P("y", SEQ),
        P("y", SEQ),
        P("y", None, None),
        P(None, "y"),
        P("y"),
        P("y", None),
        P(),
    )
    return jax.shard_map(body, mesh=whole, in_specs=placed, out_specs=P("y", SEQ, None), check_vma=False)
```
